512 devices in a mesh: slab: 512 (over x, z, y, core).
Axes of the slice: x: 4, y: 8, z: 8, core: 2. Of those that a mesh axis runs over, the one named last changes fastest.
Arguments:
- skull_state: float32 [6, 4096, 4096], P(None, 'slab'), may hold values from -6 to 6
- stiffness: float32 [4096, 4096], P('slab'), may hold values from 0.15 to 0.45
- intersection_src: int32 [131072, 4], P('slab'), may hold values from 0 to 12287
- intersection_weight: float32 [131072, 4], P('slab'), may hold values from 0.05 to 1
- brain_vel: float32 [3, 1048576], P(None, 'slab'), may hold values from -6 to 6
- connectivity: int32 [8, 1048576], P(None, 'slab'), may hold values from 0 to 2303
- region: int32 [1048576], P('slab'), may hold values from 0 to 4
- shear_table: float32 [4], replicated, may hold values from 1 to 10
- bulk_table: float32 [4], replicated, may hold values from 2 to 20
- prony_weight: float32 [12, 4], replicated, may hold values from 0.05 to 0.5
- prony_tau: float32 [12], replicated, may hold values from 0.05 to 20
- prony_state: float32 [12, 6, 1048576], P(None, None, 'slab'), may hold values from -6 to 6
- node_mass: float32 [1048576], P('slab'), may hold values from 0.5 to 2
Outputs:
- skull_out: float32 [6, 4096, 4096], P(None, 'slab')
- brain_out: float32 [3, 1048576], P(None, 'slab')
- prony_out: float32 [12, 6, 1048576], P(None, None, 'slab')
The draws below stay inside these ranges and needn't reach their ends.
Inputs may be any that keep to these rules, and one draw needn't show every extreme that they name: `intersection_src`: values are slot*4096+lane. `region`: 4 marks an empty slot.
All inputs are finite; a program needn't handle non-finite values.
Results may differ from the reference program's by a relative error of at most 0.0003.
Values sent between devices are 32-bit elements; how exact they have to be, the bound alone decides.
No kernel may reach another device: no remote copies, remote signals or barrier semaphores. Data moves between devices by JAX's collectives and lax.ppermute only.
A program may use at most 64 MiB of HBM per device.

```python
import math
import jax
import jax.numpy as jnp
import numpy as np
from jax import lax

LAYERS = 8
LANES = 4096
ELEMS = 2048
SUBSTEPS = 8
TERMS = 12
INTERSECTIONS = 4
REGIONS = 4
NODES = 2048
SHARED = 256
IFACE = 256
SKULL_ROWS = 4096
ALL_ELEMS = 1048576
ALL_NODES = 1048576
ALL_IFACE = 131072
N_SLAB = 512


def place_ends(array, own_key, low, high):
    index_at = [jax.random.randint(jax.random.fold_in(own_key, axis), (), 0, length) for axis, length in enumerate(array.shape)]
    longest = array.shape.index(max(array.shape))
    neighbour = index_at[:longest] + [(index_at[longest] + 1) % array.shape[longest]] + index_at[longest + 1:]
    return array.at[tuple(index_at)].set(low).at[tuple(neighbour)].set(high)


def shard_levels(key, extent, shards, smallest, largest):
    gain = 1.0
    for position, blocks in shards:
        steps = jax.random.uniform(jax.random.fold_in(jax.random.fold_in(key, 6), position), (blocks,), jnp.float32, smallest / len(shards), largest / len(shards))
        gain = gain * jnp.repeat(jnp.exp(steps), extent[position] // blocks).reshape((-1,) + (1,) * (len(extent) - 1 - position))
    return gain


def gaussian(stream_key, extent, deviation, most, cuts=(), held_as=jnp.bfloat16):
    drawn = deviation * jax.random.normal(stream_key, extent, jnp.float32)
    if cuts:
        drawn = drawn * shard_levels(stream_key, extent, cuts, -0.22, 0.18)
    return jnp.clip(drawn, -most, most).astype(held_as)


def setup_inputs(seed: int = 0) -> dict:
    splits = jax.random.split(jax.random.key(seed), 14)
    return {
        "skull_state": gaussian(splits[0], (6, SKULL_ROWS, LANES), 1.0, 6.0, ((1, 512),), jnp.float32),
        "stiffness": jnp.clip(0.15 + 0.29999998 * jax.random.uniform(splits[1], (SKULL_ROWS, LANES), jnp.float32) ** shard_levels(splits[1], (SKULL_ROWS, LANES), ((0, 512),), -0.2, 0.2), 0.15, 0.45),
        "intersection_src": place_ends(jax.random.randint(splits[2], (ALL_IFACE, INTERSECTIONS), 0, 3 * LANES), jax.random.fold_in(splits[2], 1), 0, (3 * LANES) - 1).astype(jnp.int32),
        "intersection_weight": jnp.clip(0.05 + 0.95 * jax.random.uniform(splits[3], (ALL_IFACE, INTERSECTIONS), jnp.float32) ** shard_levels(splits[3], (ALL_IFACE, INTERSECTIONS), ((0, 512),), -0.2, 0.2), 0.05, 1.0),
        "brain_vel": gaussian(splits[4], (3, ALL_NODES), 1.0, 6.0, ((1, 512),), jnp.float32),
        "connectivity": place_ends(jax.random.randint(splits[5], (8, ALL_ELEMS), 0, NODES + SHARED), jax.random.fold_in(splits[5], 1), 0, (NODES + SHARED) - 1).astype(jnp.int32),
        "region": place_ends(jax.random.randint(splits[6], (ALL_ELEMS,), 0, REGIONS + 1), jax.random.fold_in(splits[6], 1), 0, REGIONS).astype(jnp.int32),
        "shear_table": jnp.clip(jnp.exp(jax.random.uniform(splits[7], (REGIONS,), jnp.float32, math.log(1.0), math.log(10.0))), 1.0, 10.0),
        "bulk_table": jnp.clip(jnp.exp(jax.random.uniform(splits[8], (REGIONS,), jnp.float32, math.log(2.0), math.log(20.0))), 2.0, 20.0),
        "prony_weight": jnp.clip(jnp.exp(jax.random.uniform(splits[9], (TERMS, REGIONS), jnp.float32, math.log(0.05), math.log(0.5))), 0.05, 0.5),
        "prony_tau": jnp.clip(jnp.exp(jax.random.uniform(splits[10], (TERMS,), jnp.float32, math.log(0.05), math.log(20.0))), 0.05, 20.0),
        "prony_state": gaussian(splits[11], (TERMS, 6, ALL_ELEMS), 1.0, 6.0, ((2, 512),), jnp.float32),
        "node_mass": jnp.clip(jnp.exp(math.log(2.0) - 1.3862944 * jax.random.uniform(splits[12], (ALL_NODES,), jnp.float32) ** shard_levels(splits[12], (ALL_NODES,), ((0, 512),), -0.2, 0.2)), 0.5, 2.0),
    }


STEP_SKULL = 1.0
DAMPING = 0.05
STEP_BRAIN = 0.2
COUPLING = 0.5


def strain_table():
    table = np.zeros((6, 24), np.float32)
    for corner in range(8):
        slopes = [0.25 * (((corner >> direction) & 1) * 2 - 1) for direction in range(3)]
        table[0, corner] = slopes[0]
        table[1, 8 + corner] = slopes[1]
        table[2, 16 + corner] = slopes[2]
        table[3, corner] = slopes[1]
        table[3, 8 + corner] = slopes[0]
        table[4, 8 + corner] = slopes[2]
        table[4, 16 + corner] = slopes[1]
        table[5, corner] = slopes[2]
        table[5, 16 + corner] = slopes[0]
    return jnp.asarray(table)


def advance(padded, velocity, stiffs):
    displace = padded[:, 1:-1]
    laplace = padded[:, 2:] + padded[:, :-2] + jnp.roll(displace, 1, 2) + jnp.roll(displace, -1, 2) - 4.0 * displace
    velocity = velocity + STEP_SKULL * (stiffs * laplace - DAMPING * velocity)
    return displace + STEP_SKULL * velocity, velocity


def element_forces(corners, region, shear_table, bulk_table, prony_weight, prony_tau, prony_state):
    table = strain_table()
    high = lax.Precision.HIGHEST
    rate = jnp.dot(table, corners.reshape(24, -1), precision=high)
    strain = STEP_BRAIN * rate
    trace = strain[0] + strain[1] + strain[2]
    deviator = jnp.concatenate([strain[:3] - trace[None] / 3.0, 0.5 * strain[3:]], 0)
    labels = jnp.arange(shear_table.shape[0], dtype=jnp.int32)
    onehot = (region[None, :] == labels[:, None]).astype(strain.dtype)
    shear = jnp.dot(shear_table[None], onehot, precision=high)[0]
    bulk = jnp.dot(bulk_table[None], onehot, precision=high)[0]
    weights = jnp.dot(prony_weight, onehot, precision=high)
    live = jnp.sum(onehot, 0)
    decay = jnp.exp(-STEP_BRAIN / prony_tau)
    factor = (1.0 - decay) * prony_tau / STEP_BRAIN
    memory = decay[:, None, None] * prony_state + (2.0 * shear[None] * weights * factor[:, None])[:, None, :] * deviator[None]
    stress = jnp.sum(memory, 0) + 2.0 * shear[None] * deviator
    stress = stress.at[:3].add((bulk * trace)[None])
    stress = stress * live[None]
    forces = -jnp.dot(table.T, stress, precision=high)
    return forces.reshape(3, 8, -1), memory


def reference(skull_state, stiffness, intersection_src, intersection_weight, brain_vel, connectivity, region, shear_table, bulk_table, prony_weight, prony_tau, prony_state, node_mass):
    displace, velocity = skull_state[:3], skull_state[3:]
    kept = []
    for substep in range(SUBSTEPS):
        padded = jnp.pad(displace, ((0, 0), (1, 1), (0, 0)))
        displace, velocity = advance(padded, velocity, stiffness)
        kept.append(velocity[:, LAYERS - 1::LAYERS, :])
    history = jnp.pad(jnp.stack(kept), ((0, 0), (0, 0), (1, 1), (0, 0)))
    history = history.reshape(3 * SUBSTEPS, (N_SLAB + 2) * LANES)
    owner = (jnp.arange(ALL_IFACE, dtype=jnp.int32) // IFACE) * LANES
    columns = owner[:, None] + intersection_src
    taken = history[:, columns]
    normed = intersection_weight / jnp.sum(intersection_weight, 1, keepdims=True)
    moved = jnp.sum(taken * normed[None], -1).reshape(SUBSTEPS, 3, ALL_IFACE)
    coeffs = (jnp.arange(SUBSTEPS, dtype=jnp.float32) + 1.0) / 36.0
    target = jnp.sum(moved * coeffs[:, None, None].astype(moved.dtype), 0)
    element_owner = jnp.arange(ALL_ELEMS, dtype=jnp.int32) // ELEMS
    global_index = element_owner[None, :] * NODES + connectivity
    padded_vel = jnp.pad(brain_vel, ((0, 0), (0, SHARED)))
    corners = padded_vel[:, global_index]
    forces, memory = element_forces(corners, region, shear_table, bulk_table, prony_weight, prony_tau, prony_state)
    summed = jnp.zeros((3, ALL_NODES + SHARED), brain_vel.dtype).at[:, global_index.reshape(-1)].add(forces.reshape(3, -1))[:, :ALL_NODES]
    updated = brain_vel + STEP_BRAIN * summed / node_mass[None]
    updated = updated.reshape(3, N_SLAB, NODES)
    former = brain_vel.reshape(3, N_SLAB, NODES)[:, :, NODES - IFACE:]
    updated = updated.at[:, :, NODES - IFACE:].add(COUPLING * (target.reshape(3, N_SLAB, IFACE) - former))
    skull_out = jnp.concatenate([displace, velocity], 0)
    return skull_out, updated.reshape(3, ALL_NODES), memory
```

```python
import jax
import jax.numpy as jnp
import numpy as np
from jax import lax
from jax.experimental import pallas as pl
from jax.experimental.pallas import tpu as pltpu
from jax.sharding import PartitionSpec as P

SUBSTEPS = 8
SHARED = 256
STEP_BRAIN = 0.2
DAMPING = 0.05
COUPLING = 0.5
EDGE = 128
DEEP = 24
GROUP = 8
LO = 256
HI = 16


def strain_rows():
    table = np.zeros((16, 32), np.float32)
    for corner in range(8):
        slopes = [0.25 * ((corner >> direction & 1) * 2 - 1) for direction in range(3)]
        table[0, corner] = slopes[0]
        table[1, 8 + corner] = slopes[1]
        table[2, 16 + corner] = slopes[2]
        table[3, corner] = slopes[1]
        table[3, 8 + corner] = slopes[0]
        table[4, 8 + corner] = slopes[2]
        table[4, 16 + corner] = slopes[1]
        table[5, corner] = slopes[2]
        table[5, 16 + corner] = slopes[0]
    return table


def lookup(row, lane):
    return jnp.take_along_axis(
        jnp.broadcast_to(row, lane.shape), lane, axis=1, mode="promise_in_bounds"
    )


def pack_kernel(state, stiff, vel, out, nodes, shared, sems):
    lanes = state.shape[2]
    fetch = pltpu.make_async_copy(vel.at[:, 0:SHARED], nodes, sems.at[0])
    copies = [
        pltpu.make_async_copy(state, out.at[0:6, :, 0:lanes], sems.at[1]),
        pltpu.make_async_copy(stiff, out.at[6, :, 0:lanes], sems.at[2]),
    ]
    fetch.start()
    for copy in copies:
        copy.start()
    shared[...] = jnp.zeros((7, 8, EDGE), jnp.float32)
    fetch.wait()
    for c in range(3):
        for half in range(2):
            shared[c, half : half + 1, :] = nodes[c : c + 1, half * 128 : half * 128 + 128]
    copies.append(pltpu.make_async_copy(shared, out.at[:, :, lanes:], sems.at[3]))
    copies[-1].start()
    for copy in copies:
        copy.wait()


def is_odd():
    return lax.rem(lax.axis_index("slab"), 2) == 1


def fill(d, v, k, state, stiff, got_b, got_a, slabs):
    columns = state.shape[2] // 128
    odd = is_odd()

    def column(j, carry):
        here = pl.ds(pl.multiple_of(j * 128, 128), 128)
        for c in range(7):
            if slabs != [1]:
                a, b = got_a[c, :, here], got_b[c, :, here]
            for slab in slabs:
                if slab == 1:
                    value = state[c, :, here] if c < 6 else stiff[:, here]
                else:
                    value = jnp.where(odd, a, b) if slab == 0 else jnp.where(odd, b, a)
                at = slab * 8
                if c < 3:
                    d[pl.ds(pl.multiple_of((c * (columns + 2) + 1 + j) * DEEP + at, 8), 8), :] = value
                elif c < 6:
                    v[pl.ds(pl.multiple_of(((c - 3) * columns + j) * DEEP + at, 8), 8), :] = value
                else:
                    k[pl.ds(pl.multiple_of(j * DEEP + at, 8), 8), :] = value
        return carry

    lax.fori_loop(0, columns, column, 0, unroll=2)
    wrap(d, columns)


def wrap(d, columns):
    for c in range(3):
        base = c * (columns + 2) * DEEP
        d[base : base + DEEP, :] = d[base + columns * DEEP : base + (columns + 1) * DEEP, :]
        end = base + (columns + 1) * DEEP
        d[end : end + DEEP, :] = d[base + DEEP : base + 2 * DEEP, :]


def advance(d, v, k, windows, columns, emit):
    lane = lax.broadcasted_iota(jnp.int32, (8, 128), 1)
    first, last = lane == 0, lane == 127

    def group(g, carry):
        def at(ref, column, row):
            start = pl.multiple_of(g * (GROUP * DEEP), 8) + (column * DEEP + row)
            return ref[pl.ds(start, 8), :]

        for w in windows:
            stiffs = [at(k, i, w) for i in range(GROUP)]
            ready = []
            for c in range(3):
                base = c * (columns + 2)
                middles = [at(d, base + i, w) for i in range(GROUP + 2)]
                ahead = [pltpu.roll(m, 1, 1) for m in middles[:-1]]
                behind = [pltpu.roll(m, 127, 1) for m in middles[1:]]
                for i in range(GROUP):
                    left = jnp.where(first, ahead[i], ahead[i + 1])
                    right = jnp.where(last, behind[i + 1], behind[i])
                    middle = middles[i + 1]
                    above = at(d, base + i + 1, w - 1)
                    below = at(d, base + i + 1, w + 1)
                    laplace = (below + above) + (left + right) - 4.0 * middle
                    old = at(v, c * columns + i, w)
                    new = old + (stiffs[i] * laplace - DAMPING * old)
                    ready.append((w, c, g, i, middle + new, new))
            for item in ready:
                emit(*item)
        return carry

    lax.fori_loop(0, columns // GROUP, group, 0)


def keep(d, v, columns):
    def emit(w, c, g, i, new_d, new_v):
        base = pl.multiple_of(g * (GROUP * DEEP), 8)
        d[pl.ds(base + ((c * (columns + 2) + 1 + i) * DEEP + w), 8), :] = new_d
        v[pl.ds(base + ((c * columns + i) * DEEP + w), 8), :] = new_v

    return emit


WHOLE = [[1, 9, 15], [2, 10, 14], [3, 11, 13], [4, 12], [5, 11], [6, 10], [7, 9], [8]]
CONE = [[8, 15], [9, 14], [10, 13], [11, 12], [12], [12], [12], [12]]


def skull_kernel(state, stiff, got_b, got_a, out, d0, v0, d1, v1, k):
    columns = state.shape[2] // 128
    fill(d0, v0, k, state, stiff, got_b, got_a, [0, 1, 2])
    now, later = (d0, v0), (d1, v1)

    def last(w, c, g, i, new_d, new_v):
        here = pl.ds(pl.multiple_of(g * (GROUP * 128), 128) + i * 128, 128)
        out[c, :, here] = new_d
        out[3 + c, :, here] = new_v

    for step in range(SUBSTEPS):
        ends = step == SUBSTEPS - 1
        advance(*now, k, WHOLE[step], columns, last if ends else keep(*later, columns))
        if not ends:
            wrap(later[0], columns)
        now, later = later, now


def cone_kernel(state, stiff, got_b, got_a, shared, send, d0, v0, d1, v1, k):
    columns = state.shape[2] // 128
    fill(d0, v0, k, state, stiff, got_b, got_a, [0, 1, 2])
    now, later = (d0, v0), (d1, v1)
    for c in range(3):
        for half in range(2):
            send[c, columns + half : columns + half + 1, :] = shared[c : c + 1, half * 128 : half * 128 + 128]
    for step in range(SUBSTEPS):
        advance(*now, k, CONE[step], columns, keep(*later, columns))
        if step < SUBSTEPS - 1:
            wrap(later[0], columns)
        now, later = later, now
        for c in range(3):
            row = now[1][pl.ds(c * columns * DEEP + 15, columns, stride=DEEP), :]
            part = ((step + 1.0) / 36.0) * row
            send[c, 0:columns, :] = part if step == 0 else send[c, 0:columns, :] + part


def corners_kernel(vel, conn, out):
    blocks = conn.shape[1] // 128
    tables = vel.shape[1] // 128

    def block(b, carry):
        here = pl.ds(pl.multiple_of(b * 128, 128), 128)
        node = conn[:, here]
        lane, row = node & 127, node >> 7
        found = [jnp.zeros((8, 128), jnp.float32) for _ in range(3)]
        for r in range(tables):
            mine = row == r
            for c in range(3):
                value = lookup(vel[c : c + 1, r * 128 : r * 128 + 128], lane)
                found[c] = jnp.where(mine, value, found[c])
        for c in range(3):
            out[c * 8 : c * 8 + 8, here] = found[c]
        out[24:32, here] = jnp.zeros((8, 128), jnp.float32)
        return carry

    lax.fori_loop(0, blocks, block, 0)


def in_parts(value, count):
    parts = []
    for _ in range(count):
        part = value.astype(jnp.bfloat16)
        value = value - part.astype(jnp.float32)
        parts.append(part)
    return parts


def hexes_kernel(
    got_b, got_a, corners, conn, region, strain, spread, shear, bulk, weight, tau, memory_in,
    memory, owned, shared,
    work, rate, gains,
):
    lanes = got_a.shape[2] - EDGE
    elems = conn.shape[1]
    terms = memory_in.shape[0]
    regions = shear.shape[0]
    odd = is_odd()
    blocks = elems // 128
    first = owned.shape[1] // 128

    def add_shared(b, carry):
        here = pl.ds(pl.multiple_of(b * 128, 128), 128)
        node = conn[:, here]
        lane, row = node & 127, node >> 7
        for c in range(3):
            found = corners[c * 8 : c * 8 + 8, here]
            for half in range(2):
                a = got_a[c, half : half + 1, lanes:]
                b_ = got_b[c, half : half + 1, lanes:]
                found = jnp.where(row == first + half, lookup(jnp.where(odd, b_, a), lane), found)
            work[c * 8 : c * 8 + 8, here] = found
        work[24:32, here] = jnp.zeros((8, 128), jnp.float32)
        return carry

    lax.fori_loop(0, blocks, add_shared, 0, unroll=2)
    table = strain[...].astype(jnp.bfloat16)
    rate[...] = STEP_BRAIN * sum(
        jnp.dot(table, part, preferred_element_type=jnp.float32) for part in in_parts(work[...], 3)
    )

    def put(index, value):
        gains[index * 8 : index * 8 + 8, :] = jnp.broadcast_to(value, (8, 128))

    for r in range(regions):
        put(terms * regions + r, 2.0 * shear[r])
        put((terms + 1) * regions + r, bulk[r])
    for t in range(terms):
        span = jnp.full((8, 128), tau[t], jnp.float32)
        decay = jnp.exp(-STEP_BRAIN / span)
        put((terms + 2) * regions + t, decay)
        factor = (1.0 - decay) * span / STEP_BRAIN
        for r in range(regions):
            put(t * regions + r, (2.0 * shear[r] * weight[r, t]) * factor)

    def gain(index):
        return gains[index * 8 : index * 8 + 6, :]

    normal = lax.broadcasted_iota(jnp.int32, (6, 128), 0) < 3

    def block(b, carry):
        here = pl.ds(pl.multiple_of(b * 128, 128), 128)
        strains = rate[0:6, here]
        trace = rate[0:1, here] + rate[1:2, here] + rate[2:3, here]
        dev = jnp.where(normal, strains - trace / 3.0, 0.5 * strains)
        label = jnp.broadcast_to(region[:, here], (6, 128))
        masks = [label == r for r in range(regions)]

        def pick(t):
            chosen = jnp.zeros((6, 128), jnp.float32)
            for r, mask in enumerate(masks):
                chosen = jnp.where(mask, gain(t * regions + r), chosen)
            return chosen

        stress = pick(terms) * dev + jnp.where(normal, pick(terms + 1) * trace, 0.0)
        for t in range(terms):
            new = gain((terms + 2) * regions + t) * memory_in[t, :, here] + pick(t) * dev
            memory[t, :, here] = new
            stress = stress + new
        rate[0:6, here] = jnp.where(label < regions, stress, 0.0)
        return carry

    lax.fori_loop(0, blocks, block, 0, unroll=2)
    rate[6:16, :] = jnp.zeros((10, elems), jnp.float32)
    table = spread[...].astype(jnp.bfloat16)
    work[...] = sum(jnp.dot(table, part, preferred_element_type=jnp.float32) for part in in_parts(rate[...], 2))

    low_rows = lax.broadcasted_iota(jnp.int32, (LO, elems), 0)
    high_rows = lax.broadcasted_iota(jnp.int32, (HI, elems), 0)

    def corner(q, sums):
        node = conn[pl.ds(q, 1), :]
        low = (low_rows == (node & (LO - 1))).astype(jnp.float32).astype(jnp.bfloat16)
        mine = high_rows == (node >> 8)
        parts = []
        for c in range(3):
            parts += in_parts(jnp.where(mine, work[pl.ds(c * 8 + q, 1), :], 0.0), 2)
        return sums + lax.dot_general(
            jnp.concatenate(parts, 0), low, (((1,), (1,)), ((), ())), preferred_element_type=jnp.float32
        )

    sums = lax.fori_loop(0, 8, corner, jnp.zeros((6 * HI, LO), jnp.float32))
    for c in range(3):
        at = c * 2 * HI
        whole = sums[at : at + HI] + sums[at + HI : at + 2 * HI]
        for h in range(8):
            owned[c : c + 1, h * LO : h * LO + LO] = whole[h : h + 1]
        shared[c : c + 1, :] = whole[8:9]


def finish_kernel(sent, got_b, got_a, owned, vel, mass, src, weight, out):
    nodes = vel.shape[1]
    tables = sent.shape[1] - 2
    odd = is_odd()
    place = jnp.concatenate([src[:, 0:128], src[:, 128:256]], 0)
    share = weight[...] / jnp.sum(weight[...], 0, keepdims=True)
    share = jnp.concatenate([share[:, 0:128], share[:, 128:256]], 0)
    lane, row = place & 127, place >> 7
    for c in range(3):
        before = jnp.where(odd, got_a[c], got_b[c])
        after = jnp.where(odd, got_b[c], got_a[c])
        found = jnp.zeros((8, 128), jnp.float32)
        for slot, values in enumerate((before, sent[c], after)):
            for r in range(tables):
                found = jnp.where(row == slot * tables + r, lookup(values[r : r + 1], lane), found)
        found = found * share
        target = jnp.concatenate(
            [jnp.sum(found[0:4], 0, keepdims=True), jnp.sum(found[4:8], 0, keepdims=True)], 1
        )
        incoming = jnp.concatenate([before[tables : tables + 1], before[tables + 1 : tables + 2]], 1)
        old = vel[c : c + 1, :]
        total = owned[c : c + 1, :]
        total = jnp.concatenate([total[:, 0:SHARED] + incoming, total[:, SHARED:]], 1)
        new = old + STEP_BRAIN * total / mass[...]
        split = nodes - SHARED
        out[c : c + 1, 0:split] = new[:, 0:split]
        out[c : c + 1, split:] = new[:, split:] + COUPLING * (target - old[:, split:])


def on_device(
    skull_state, stiffness, intersection_src, intersection_weight, brain_vel, connectivity, region,
    shear_table, bulk_table, prony_weight, prony_tau, prony_state, node_mass,
):
    lanes = skull_state.shape[2]
    columns = lanes // 128
    nodes = brain_vel.shape[1]
    elems = connectivity.shape[1]
    terms, regions = prony_weight.shape
    count = lax.axis_size("slab")
    vmem = pl.BlockSpec(memory_space=pltpu.VMEM)
    smem = pl.BlockSpec(memory_space=pltpu.SMEM)
    hbm = pl.BlockSpec(memory_space=pltpu.HBM)
    shape = lambda *dims: jax.ShapeDtypeStruct(dims, jnp.float32)
    scratch = lambda *dims: pltpu.VMEM(dims, jnp.float32)

    def kernel(body, out, operands, results, scratch_shapes=(), flops=1_000_000, vmem_mib=32):
        return pl.pallas_call(
            body,
            out_shape=out,
            in_specs=operands,
            out_specs=results,
            scratch_shapes=list(scratch_shapes),
            compiler_params=pltpu.CompilerParams(vmem_limit_bytes=vmem_mib << 20),
            cost_estimate=pl.CostEstimate(flops=flops, bytes_accessed=4_000_000, transcendentals=0),
            name=body.__name__.removesuffix("_kernel"),
        )

    swap_a = [(i, i ^ 1) for i in range(count)]
    swap_b = [(i, ((i + 1) ^ 1) - 1) for i in range(1, count - 1)]
    field = [scratch(3 * (columns + 2) * DEEP, 128), scratch(3 * columns * DEEP, 128)]
    slabs = field + field + [scratch(columns * DEEP, 128)]
    table = strain_rows()

    package = kernel(
        pack_kernel, shape(7, 8, lanes + EDGE), [hbm, hbm, hbm], hbm,
        [scratch(3, SHARED), scratch(7, 8, EDGE), pltpu.SemaphoreType.DMA((4,))], vmem_mib=60,
    )(skull_state, stiffness, brain_vel)
    got_b = lax.ppermute(package, "slab", swap_b)
    got_a = lax.ppermute(package, "slab", swap_a)
    corners = kernel(corners_kernel, shape(32, elems), [vmem] * 2, vmem)(brain_vel, connectivity)
    memory, owned, shared = kernel(
        hexes_kernel,
        (shape(*prony_state.shape), shape(3, nodes), shape(3, SHARED)),
        [vmem] * 7 + [smem] * 4 + [vmem],
        [vmem] * 3,
        [scratch(32, elems), scratch(16, elems), scratch(((terms + 2) * regions + terms) * 8, 128)],
    )(
        got_b, got_a, corners, connectivity, region.reshape(1, elems), jnp.asarray(table), jnp.asarray(-table.T),
        shear_table, bulk_table, prony_weight.T, prony_tau, prony_state,
    )
    sent = kernel(cone_kernel, shape(3, columns + 2, 128), [vmem] * 5, vmem, slabs)(
        skull_state, stiffness, got_b, got_a, shared
    )
    back_b = lax.ppermute(sent, "slab", swap_b)
    back_a = lax.ppermute(sent, "slab", swap_a)
    skull_out = kernel(skull_kernel, shape(*skull_state.shape), [vmem] * 4, vmem, slabs, 50_000_000)(
        skull_state, stiffness, got_b, got_a
    )
    brain_out = kernel(finish_kernel, shape(3, nodes), [vmem] * 8, vmem)(
        sent, back_b, back_a, owned, brain_vel, node_mass.reshape(1, nodes), intersection_src.T, intersection_weight.T
    )
    return skull_out, brain_out, memory


def solution(mesh):
    placed = (
        P(None, "slab", None),
        P("slab", None),
        P("slab", None),
        P("slab", None),
        P(None, "slab"),
        P(None, "slab"),
        P("slab"),
        P(),
        P(),
        P(),
        P(),
        P(None, None, "slab"),
        P("slab"),
    )
    return jax.shard_map(
        on_device,
        mesh=mesh,
        in_specs=placed,
        out_specs=(P(None, "slab", None), P(None, "slab"), P(None, None, "slab")),
        check_vma=False,
    )
```

```python
import jax
import jax.numpy as jnp
import numpy as np
from jax import lax
from jax.experimental import pallas as pl
from jax.experimental.pallas import tpu as pltpu
from jax.sharding import PartitionSpec as P

SUBSTEPS = 8
SHARED = 256
STEP_BRAIN = 0.2
DAMPING = 0.05
COUPLING = 0.5
EDGE = 128
DEEP = 24
GROUP = 8
LO = 256
HI = 16


def strain_rows():
    table = np.zeros((16, 32), np.float32)
    for corner in range(8):
        slopes = [0.25 * ((corner >> direction & 1) * 2 - 1) for direction in range(3)]
        table[0, corner] = slopes[0]
        table[1, 8 + corner] = slopes[1]
        table[2, 16 + corner] = slopes[2]
        table[3, corner] = slopes[1]
        table[3, 8 + corner] = slopes[0]
        table[4, 8 + corner] = slopes[2]
        table[4, 16 + corner] = slopes[1]
        table[5, corner] = slopes[2]
        table[5, 16 + corner] = slopes[0]
    return table


def lookup(row, lane):
    return jnp.take_along_axis(
        jnp.broadcast_to(row, lane.shape), lane, axis=1, mode="promise_in_bounds"
    )


def pack_kernel(state, stiff, vel, out, nodes, package, sems):
    lanes = state.shape[2]
    first = pltpu.make_async_copy(vel.at[:, 0:SHARED], nodes, sems.at[14])
    arrive = [
        pltpu.make_async_copy(state.at[c] if c < 6 else stiff, package.at[c, :, 0:lanes], sems.at[c]) for c in range(7)
    ]
    leave = [pltpu.make_async_copy(package.at[c], out.at[c], sems.at[7 + c]) for c in range(7)]
    first.start()
    for copy in arrive:
        copy.start()
    package[:, :, lanes:] = jnp.zeros((7, 8, EDGE), jnp.float32)
    first.wait()
    for c in range(3):
        for half in range(2):
            package[c, half : half + 1, lanes:] = nodes[c : c + 1, half * 128 : half * 128 + 128]
    for c in range(7):
        arrive[c].wait()
        leave[c].start()
    for copy in leave:
        copy.wait()


def is_odd():
    return lax.rem(lax.axis_index("slab"), 2) == 1


def from_previous(by_b, by_a):
    return jnp.where(is_odd(), by_a, by_b)


def from_next(by_b, by_a):
    return jnp.where(is_odd(), by_b, by_a)


def fill(d, v, k, state, stiff, got_a, got_b):
    columns = state.shape[2] // 128

    def column(j, carry):
        here = pl.ds(pl.multiple_of(j * 128, 128), 128)
        for c in range(7):
            own = state[c, :, here] if c < 6 else stiff[:, here]
            b, a = got_b[c, :, here], got_a[c, :, here]
            for slab, value in enumerate((from_previous(b, a), own, from_next(b, a))):
                at = slab * 8
                if c < 3:
                    d[pl.ds(pl.multiple_of((c * (columns + 2) + 1 + j) * DEEP + at, 8), 8), :] = value
                elif c < 6:
                    v[pl.ds(pl.multiple_of(((c - 3) * columns + j) * DEEP + at, 8), 8), :] = value
                else:
                    k[pl.ds(pl.multiple_of(j * DEEP + at, 8), 8), :] = value
        return carry

    lax.fori_loop(0, columns, column, 0, unroll=2)
    wrap(d, columns)


def wrap(d, columns):
    for c in range(3):
        base = c * (columns + 2) * DEEP
        d[base : base + DEEP, :] = d[base + columns * DEEP : base + (columns + 1) * DEEP, :]
        end = base + (columns + 1) * DEEP
        d[end : end + DEEP, :] = d[base + DEEP : base + 2 * DEEP, :]


def advance(d, v, k, windows, columns, emit):
    lane = lax.broadcasted_iota(jnp.int32, (8, 128), 1)
    first, last = lane == 0, lane == 127

    def group(g, carry):
        def at(ref, column, row):
            start = pl.multiple_of(g * (GROUP * DEEP), 8) + (column * DEEP + row)
            return ref[pl.ds(start, 8), :]

        for w in windows:
            stiffs = [at(k, i, w) for i in range(GROUP)]
            ready = []
            for c in range(3):
                base = c * (columns + 2)
                middles = [at(d, base + i, w) for i in range(GROUP + 2)]
                ahead = [pltpu.roll(m, 1, 1) for m in middles[:-1]]
                behind = [pltpu.roll(m, 127, 1) for m in middles[1:]]
                for i in range(GROUP):
                    left = jnp.where(first, ahead[i], ahead[i + 1])
                    right = jnp.where(last, behind[i + 1], behind[i])
                    middle = middles[i + 1]
                    above = at(d, base + i + 1, w - 1)
                    below = at(d, base + i + 1, w + 1)
                    laplace = (below + above) + (left + right) - 4.0 * middle
                    old = at(v, c * columns + i, w)
                    new = old + (stiffs[i] * laplace - DAMPING * old)
                    ready.append((w, c, g, i, middle + new, new))
            for item in ready:
                emit(*item)
        return carry

    lax.fori_loop(0, columns // GROUP, group, 0)


def keep(d, v, columns):
    def emit(w, c, g, i, new_d, new_v):
        base = pl.multiple_of(g * (GROUP * DEEP), 8)
        d[pl.ds(base + ((c * (columns + 2) + 1 + i) * DEEP + w), 8), :] = new_d
        v[pl.ds(base + ((c * columns + i) * DEEP + w), 8), :] = new_v

    return emit


WHOLE = [[1, 9, 15], [2, 10, 14], [3, 11, 13], [4, 12], [5, 11], [6, 10], [7, 9], [8]]


def skull_kernel(state, stiff, got_a, got_b, shared, out, send, d0, v0, d1, v1, k):
    columns = state.shape[2] // 128
    fill(d0, v0, k, state, stiff, got_a, got_b)
    now, later = (d0, v0), (d1, v1)
    for c in range(3):
        for half in range(2):
            send[c, columns + half : columns + half + 1, :] = shared[c : c + 1, half * 128 : half * 128 + 128]

    def last(w, c, g, i, new_d, new_v):
        here = pl.ds(pl.multiple_of(g * (GROUP * 128), 128) + i * 128, 128)
        out[c, :, here] = new_d
        out[3 + c, :, here] = new_v
        base = pl.multiple_of(g * (GROUP * DEEP), 8)
        v0[pl.ds(base + ((c * columns + i) * DEEP + w), 8), :] = new_v

    for step in range(SUBSTEPS):
        ends = step == SUBSTEPS - 1
        advance(*now, k, WHOLE[step], columns, last if ends else keep(*later, columns))
        if not ends:
            wrap(later[0], columns)
        now, later = later, now
        for c in range(3):
            row = now[1][pl.ds(c * columns * DEEP + 15, columns, stride=DEEP), :]
            part = ((step + 1.0) / 36.0) * row
            send[c, 0:columns, :] = part if step == 0 else send[c, 0:columns, :] + part


def prepare_kernel(vel, conn, src, weight, shear, bulk, prony, tau, out, place, share, gains, lows):
    elems = conn.shape[1]
    regions, terms = prony.shape
    normed = weight[...] / jnp.sum(weight[...], 0, keepdims=True)
    for half in range(2):
        place[half * 4 : half * 4 + 4, :] = src[:, half * 128 : half * 128 + 128]
        share[half * 4 : half * 4 + 4, :] = normed[:, half * 128 : half * 128 + 128]

    def put(index, value):
        gains[index * 8 : index * 8 + 8, :] = jnp.broadcast_to(value, (8, 128))

    for r in range(regions):
        put(terms * regions + r, 2.0 * shear[r])
        put((terms + 1) * regions + r, bulk[r])
    for t in range(terms):
        span = jnp.full((8, 128), tau[t], jnp.float32)
        decay = jnp.exp(-STEP_BRAIN / span)
        put((terms + 2) * regions + t, decay)
        factor = (1.0 - decay) * span / STEP_BRAIN
        for r in range(regions):
            put(t * regions + r, (2.0 * shear[r] * prony[r, t]) * factor)

    low_rows = lax.broadcasted_iota(jnp.int32, (LO, elems), 0)

    def corner(q, carry):
        node = conn[pl.ds(q, 1), :]
        lows[q] = (low_rows == (node & (LO - 1))).astype(jnp.float32).astype(jnp.bfloat16)
        return carry

    lax.fori_loop(0, 8, corner, 0)
    blocks = conn.shape[1] // 128
    tables = vel.shape[1] // 128

    def block(b, carry):
        here = pl.ds(pl.multiple_of(b * 128, 128), 128)
        node = conn[:, here]
        lane, row = node & 127, node >> 7
        found = [jnp.zeros((8, 128), jnp.float32) for _ in range(3)]
        for r in range(tables):
            mine = row == r
            for c in range(3):
                value = lookup(vel[c : c + 1, r * 128 : r * 128 + 128], lane)
                found[c] = jnp.where(mine, value, found[c])
        for c in range(3):
            out[c * 8 : c * 8 + 8, here] = found[c]
        out[24:32, here] = jnp.zeros((8, 128), jnp.float32)
        return carry

    lax.fori_loop(0, blocks, block, 0)


def in_parts(value, count):
    parts = []
    for _ in range(count):
        part = value.astype(jnp.bfloat16)
        value = value - part.astype(jnp.float32)
        parts.append(part)
    return parts


def hexes_kernel(
    got_a, got_b, corners, conn, region, strain, spread, vel, mass, memory_in, gains, lows,
    memory, base, shared, scale,
    work, rate,
):
    elems = conn.shape[1]
    terms = memory_in.shape[0]
    regions = (gains.shape[0] // 8 - terms) // (terms + 2)
    blocks = elems // 128
    lanes = got_b.shape[2] - EDGE
    ghost = from_next(got_b[0:3, :, lanes:], got_a[0:3, :, lanes:])
    first = base.shape[1] // 128

    def add_shared(b, carry):
        here = pl.ds(pl.multiple_of(b * 128, 128), 128)
        node = conn[:, here]
        lane, row = node & 127, node >> 7
        for c in range(3):
            found = corners[c * 8 : c * 8 + 8, here]
            for half in range(2):
                value = lookup(ghost[c, half : half + 1], lane)
                found = jnp.where(row == first + half, value, found)
            work[c * 8 : c * 8 + 8, here] = found
        work[24:32, here] = jnp.zeros((8, 128), jnp.float32)
        return carry

    lax.fori_loop(0, blocks, add_shared, 0, unroll=2)
    table = strain[...].astype(jnp.bfloat16)
    rate[...] = STEP_BRAIN * sum(
        jnp.dot(table, part, preferred_element_type=jnp.float32) for part in in_parts(work[...], 3)
    )

    def gain(index):
        return gains[index * 8 : index * 8 + 6, :]

    normal = lax.broadcasted_iota(jnp.int32, (6, 128), 0) < 3

    def block(b, carry):
        here = pl.ds(pl.multiple_of(b * 128, 128), 128)
        strains = rate[0:6, here]
        trace = rate[0:1, here] + rate[1:2, here] + rate[2:3, here]
        dev = jnp.where(normal, strains - trace / 3.0, 0.5 * strains)
        label = jnp.broadcast_to(region[:, here], (6, 128))
        masks = [label == r for r in range(regions)]

        def pick(t):
            chosen = jnp.zeros((6, 128), jnp.float32)
            for r, mask in enumerate(masks):
                chosen = jnp.where(mask, gain(t * regions + r), chosen)
            return chosen

        stress = pick(terms) * dev + jnp.where(normal, pick(terms + 1) * trace, 0.0)
        for t in range(terms):
            new = gain((terms + 2) * regions + t) * memory_in[t, :, here] + pick(t) * dev
            memory[t, :, here] = new
            stress = stress + new
        rate[0:6, here] = jnp.where(label < regions, stress, 0.0)
        return carry

    lax.fori_loop(0, blocks, block, 0, unroll=2)
    rate[6:16, :] = jnp.zeros((10, elems), jnp.float32)
    table = spread[...].astype(jnp.bfloat16)
    work[...] = sum(jnp.dot(table, part, preferred_element_type=jnp.float32) for part in in_parts(rate[...], 2))

    high_rows = lax.broadcasted_iota(jnp.int32, (HI, elems), 0)

    def corner(q, sums):
        node = conn[pl.ds(q, 1), :]
        mine = high_rows == (node >> 8)
        parts = []
        for c in range(3):
            parts += in_parts(jnp.where(mine, work[pl.ds(c * 8 + q, 1), :], 0.0), 2)
        return sums + lax.dot_general(
            jnp.concatenate(parts, 0), lows[q], (((1,), (1,)), ((), ())), preferred_element_type=jnp.float32
        )

    sums = lax.fori_loop(0, 8, corner, jnp.zeros((6 * HI, LO), jnp.float32))
    for c in range(3):
        at = c * 2 * HI
        whole = sums[at : at + HI] + sums[at + HI : at + 2 * HI]
        for h in range(8):
            here = slice(h * LO, h * LO + LO)
            old = vel[c : c + 1, here]
            base[c : c + 1, here] = old * (1.0 - COUPLING if h == 7 else 1.0) + STEP_BRAIN * whole[h : h + 1] / mass[:, here]
        shared[c : c + 1, :] = whole[8:9]
    scale[...] = STEP_BRAIN / mass[:, 0:SHARED]


def finish_kernel(sent, got_a, got_b, base, scale, place, share, out):
    nodes = base.shape[1]
    tables = sent.shape[1] - 2
    lane, row = place[...] & 127, place[...] >> 7
    for c in range(3):
        before = from_previous(got_b[c], got_a[c])
        after = from_next(got_b[c], got_a[c])
        found = jnp.zeros((8, 128), jnp.float32)
        for slot, values in enumerate((before, sent[c], after)):
            for r in range(tables):
                found = jnp.where(row == slot * tables + r, lookup(values[r : r + 1], lane), found)
        found = found * share[...]
        target = jnp.concatenate(
            [jnp.sum(found[0:4], 0, keepdims=True), jnp.sum(found[4:8], 0, keepdims=True)], 1
        )
        incoming = jnp.concatenate([before[tables : tables + 1], before[tables + 1 : tables + 2]], 1)
        split = nodes - SHARED
        out[c : c + 1, 0:SHARED] = base[c : c + 1, 0:SHARED] + incoming * scale[...]
        out[c : c + 1, SHARED:split] = base[c : c + 1, SHARED:split]
        out[c : c + 1, split:] = base[c : c + 1, split:] + COUPLING * target


def on_device(
    skull_state, stiffness, intersection_src, intersection_weight, brain_vel, connectivity, region,
    shear_table, bulk_table, prony_weight, prony_tau, prony_state, node_mass,
):
    lanes = skull_state.shape[2]
    columns = lanes // 128
    nodes = brain_vel.shape[1]
    elems = connectivity.shape[1]
    terms, regions = prony_weight.shape
    count = lax.axis_size("slab")
    vmem = pl.BlockSpec(memory_space=pltpu.VMEM)
    smem = pl.BlockSpec(memory_space=pltpu.SMEM)
    hbm = pl.BlockSpec(memory_space=pltpu.HBM)
    shape = lambda *dims: jax.ShapeDtypeStruct(dims, jnp.float32)
    scratch = lambda *dims: pltpu.VMEM(dims, jnp.float32)

    def kernel(body, out, operands, results, scratch_shapes=(), flops=1_000_000, vmem_mib=32):
        return pl.pallas_call(
            body,
            out_shape=out,
            in_specs=operands,
            out_specs=results,
            scratch_shapes=list(scratch_shapes),
            compiler_params=pltpu.CompilerParams(vmem_limit_bytes=vmem_mib << 20),
            cost_estimate=pl.CostEstimate(flops=flops, bytes_accessed=4_000_000, transcendentals=0),
            name=body.__name__.removesuffix("_kernel"),
        )

    swap_a = [(i, i ^ 1) for i in range(count)]
    swap_b = [(i, ((i + 1) ^ 1) - 1) for i in range(1, count - 1)]

    def swap(value):
        return lax.ppermute(value, "slab", swap_b), lax.ppermute(value, "slab", swap_a)

    field = [scratch(3 * (columns + 2) * DEEP, 128), scratch(3 * columns * DEEP, 128)]
    slabs = field + field + [scratch(columns * DEEP, 128)]
    table = strain_rows()

    package = kernel(
        pack_kernel, shape(7, 8, lanes + EDGE), [hbm, hbm, hbm], hbm,
        [scratch(3, SHARED), scratch(7, 8, lanes + EDGE), pltpu.SemaphoreType.DMA((15,))], vmem_mib=60,
    )(skull_state, stiffness, brain_vel)
    got_b, got_a = swap(package)
    gain_rows = ((terms + 2) * regions + terms) * 8
    corners, place, share, gains, lows = kernel(
        prepare_kernel,
        (
            shape(32, elems),
            jax.ShapeDtypeStruct((8, 128), jnp.int32),
            shape(8, 128),
            shape(gain_rows, 128),
            jax.ShapeDtypeStruct((8, LO, elems), jnp.bfloat16),
        ),
        [vmem] * 4 + [smem] * 4,
        [vmem] * 5,
    )(
        brain_vel, connectivity, intersection_src.T, intersection_weight.T,
        shear_table, bulk_table, prony_weight.T, prony_tau,
    )
    memory, base, shared, scale = kernel(
        hexes_kernel,
        (shape(*prony_state.shape), shape(3, nodes), shape(3, SHARED), shape(1, SHARED)),
        [vmem] * 12,
        [vmem] * 4,
        [scratch(32, elems), scratch(16, elems)],
    )(
        got_a, got_b, corners, connectivity, region.reshape(1, elems), jnp.asarray(table), jnp.asarray(-table.T),
        brain_vel, node_mass.reshape(1, nodes), prony_state, gains, lows,
    )
    skull_out, sent = kernel(
        skull_kernel,
        (shape(*skull_state.shape), shape(3, columns + 2, 128)),
        [vmem] * 5,
        [vmem] * 2,
        slabs,
    )(skull_state, stiffness, got_a, got_b, shared)
    back_b, back_a = swap(sent)
    brain_out = kernel(finish_kernel, shape(3, nodes), [vmem] * 7, vmem)(
        sent, back_a, back_b, base, scale, place, share
    )
    return skull_out, brain_out, memory


def solution(mesh):
    placed = (
        P(None, "slab", None),
        P("slab", None),
        P("slab", None),
        P("slab", None),
        P(None, "slab"),
        P(None, "slab"),
        P("slab"),
        P(),
        P(),
        P(),
        P(),
        P(None, None, "slab"),
        P("slab"),
    )
    return jax.shard_map(
        on_device,
        mesh=mesh,
        in_specs=placed,
        out_specs=(P(None, "slab", None), P(None, "slab"), P(None, None, "slab")),
        check_vma=False,
    )
```

```python
import jax
import jax.numpy as jnp
import numpy as np
from jax import lax
from jax.experimental import pallas as pl
from jax.experimental.pallas import tpu as pltpu
from jax.sharding import PartitionSpec as P

SUBSTEPS = 8
SHARED = 256
STEP_BRAIN = 0.2
DAMPING = 0.05
COUPLING = 0.5
EDGE = 128
DEEP = 24
GROUP = 8
LO = 128
HI = 32


def strain_rows():
    table = np.zeros((16, 32), np.float32)
    for corner in range(8):
        slopes = [0.25 * ((corner >> direction & 1) * 2 - 1) for direction in range(3)]
        table[0, corner] = slopes[0]
        table[1, 8 + corner] = slopes[1]
        table[2, 16 + corner] = slopes[2]
        table[3, corner] = slopes[1]
        table[3, 8 + corner] = slopes[0]
        table[4, 8 + corner] = slopes[2]
        table[4, 16 + corner] = slopes[1]
        table[5, corner] = slopes[2]
        table[5, 16 + corner] = slopes[0]
    return table


def lookup(row, lane):
    return jnp.take_along_axis(
        jnp.broadcast_to(row, lane.shape), lane, axis=1, mode="promise_in_bounds"
    )


def pack_kernel(state, stiff, vel, out, nodes, package, sems):
    lanes = state.shape[2]
    first = pltpu.make_async_copy(vel.at[:, 0:SHARED], nodes, sems.at[14])
    arrive = [
        pltpu.make_async_copy(state.at[c] if c < 6 else stiff, package.at[c, :, 0:lanes], sems.at[c]) for c in range(7)
    ]
    leave = [pltpu.make_async_copy(package.at[c], out.at[c], sems.at[7 + c]) for c in range(7)]
    first.start()
    for copy in arrive:
        copy.start()
    package[:, :, lanes:] = jnp.zeros((7, 8, EDGE), jnp.float32)
    first.wait()
    for c in range(3):
        for half in range(2):
            package[c, half : half + 1, lanes:] = nodes[c : c + 1, half * 128 : half * 128 + 128]
    for c in range(7):
        arrive[c].wait()
        leave[c].start()
    for copy in leave:
        copy.wait()


def is_odd():
    return lax.rem(lax.axis_index("slab"), 2) == 1


def from_previous(by_b, by_a):
    return jnp.where(is_odd(), by_a, by_b)


def from_next(by_b, by_a):
    return jnp.where(is_odd(), by_b, by_a)


def fill(d, v, k, state, stiff, got_a, got_b):
    columns = state.shape[2] // 128

    def column(j, carry):
        here = pl.ds(pl.multiple_of(j * 128, 128), 128)
        for c in range(7):
            own = state[c, :, here] if c < 6 else stiff[:, here]
            b, a = got_b[c, :, here], got_a[c, :, here]
            for slab, value in enumerate((from_previous(b, a), own, from_next(b, a))):
                at = slab * 8
                if c < 3:
                    d[pl.ds(pl.multiple_of((c * (columns + 2) + 1 + j) * DEEP + at, 8), 8), :] = value
                elif c < 6:
                    v[pl.ds(pl.multiple_of(((c - 3) * columns + j) * DEEP + at, 8), 8), :] = value
                else:
                    k[pl.ds(pl.multiple_of(j * DEEP + at, 8), 8), :] = value
        return carry

    lax.fori_loop(0, columns, column, 0, unroll=2)
    wrap(d, columns)


def wrap(d, columns):
    for c in range(3):
        base = c * (columns + 2) * DEEP
        d[base : base + DEEP, :] = d[base + columns * DEEP : base + (columns + 1) * DEEP, :]
        end = base + (columns + 1) * DEEP
        d[end : end + DEEP, :] = d[base + DEEP : base + 2 * DEEP, :]


def advance(d, v, k, windows, columns, emit):
    lane = lax.broadcasted_iota(jnp.int32, (8, 128), 1)
    first, last = lane == 0, lane == 127

    def group(g, carry):
        def at(ref, column, row):
            start = pl.multiple_of(g * (GROUP * DEEP), 8) + (column * DEEP + row)
            return ref[pl.ds(start, 8), :]

        for w in windows:
            stiffs = [at(k, i, w) for i in range(GROUP)]
            ready = []
            for c in range(3):
                base = c * (columns + 2)
                middles = [at(d, base + i, w) for i in range(GROUP + 2)]
                ahead = [pltpu.roll(m, 1, 1) for m in middles[:-1]]
                behind = [pltpu.roll(m, 127, 1) for m in middles[1:]]
                for i in range(GROUP):
                    left = jnp.where(first, ahead[i], ahead[i + 1])
                    right = jnp.where(last, behind[i + 1], behind[i])
                    middle = middles[i + 1]
                    above = at(d, base + i + 1, w - 1)
                    below = at(d, base + i + 1, w + 1)
                    laplace = (below + above) + (left + right) - 4.0 * middle
                    old = at(v, c * columns + i, w)
                    new = old + (stiffs[i] * laplace - DAMPING * old)
                    ready.append((w, c, g, i, middle + new, new))
            for item in ready:
                emit(*item)
        return carry

    lax.fori_loop(0, columns // GROUP, group, 0)


def keep(d, v, columns):
    def emit(w, c, g, i, new_d, new_v):
        base = pl.multiple_of(g * (GROUP * DEEP), 8)
        d[pl.ds(base + ((c * (columns + 2) + 1 + i) * DEEP + w), 8), :] = new_d
        v[pl.ds(base + ((c * columns + i) * DEEP + w), 8), :] = new_v

    return emit


WHOLE = [[1, 9, 15], [2, 10, 14], [3, 11, 13], [4, 12], [5, 11], [6, 10], [7, 9], [8]]


def skull_kernel(state, stiff, got_a, got_b, shared, out, send, d0, v0, d1, v1, k):
    columns = state.shape[2] // 128
    fill(d0, v0, k, state, stiff, got_a, got_b)
    now, later = (d0, v0), (d1, v1)
    for c in range(3):
        for half in range(2):
            send[c, columns + half : columns + half + 1, :] = shared[c : c + 1, half * 128 : half * 128 + 128]

    def last(w, c, g, i, new_d, new_v):
        here = pl.ds(pl.multiple_of(g * (GROUP * 128), 128) + i * 128, 128)
        out[c, :, here] = new_d
        out[3 + c, :, here] = new_v
        base = pl.multiple_of(g * (GROUP * DEEP), 8)
        v0[pl.ds(base + ((c * columns + i) * DEEP + w), 8), :] = new_v

    for step in range(SUBSTEPS):
        ends = step == SUBSTEPS - 1
        advance(*now, k, WHOLE[step], columns, last if ends else keep(*later, columns))
        if not ends:
            wrap(later[0], columns)
        now, later = later, now
        for c in range(3):
            row = now[1][pl.ds(c * columns * DEEP + 15, columns, stride=DEEP), :]
            part = ((step + 1.0) / 36.0) * row
            send[c, 0:columns, :] = part if step == 0 else send[c, 0:columns, :] + part


def corners_kernel(vel, conn, src, weight, out, place, share):
    normed = weight[...] / jnp.sum(weight[...], 0, keepdims=True)
    for half in range(2):
        place[half * 4 : half * 4 + 4, :] = src[:, half * 128 : half * 128 + 128]
        share[half * 4 : half * 4 + 4, :] = normed[:, half * 128 : half * 128 + 128]
    blocks = conn.shape[1] // 128
    tables = vel.shape[1] // 128

    def block(b, carry):
        here = pl.ds(pl.multiple_of(b * 128, 128), 128)
        node = conn[:, here]
        lane, row = node & 127, node >> 7
        found = [jnp.zeros((8, 128), jnp.float32) for _ in range(3)]
        for r in range(tables):
            mine = row == r
            for c in range(3):
                value = lookup(vel[c : c + 1, r * 128 : r * 128 + 128], lane)
                found[c] = jnp.where(mine, value, found[c])
        for c in range(3):
            out[c * 8 : c * 8 + 8, here] = found[c]
        out[24:32, here] = jnp.zeros((8, 128), jnp.float32)
        return carry

    lax.fori_loop(0, blocks, block, 0)


def in_parts(value, count):
    parts = []
    for _ in range(count):
        part = value.astype(jnp.bfloat16)
        value = value - part.astype(jnp.float32)
        parts.append(part)
    return parts


def hexes_kernel(
    got_a, got_b, corners, conn, region, strain, spread, vel, mass, shear, bulk, weight, tau, memory_in,
    memory, base, shared, scale,
    work, rate, gains,
):
    elems = conn.shape[1]
    terms = memory_in.shape[0]
    regions = shear.shape[0]
    blocks = elems // 128
    lanes = got_b.shape[2] - EDGE
    ghost = from_next(got_b[0:3, :, lanes:], got_a[0:3, :, lanes:])
    first = base.shape[1] // 128

    def add_shared(b, carry):
        here = pl.ds(pl.multiple_of(b * 128, 128), 128)
        node = conn[:, here]
        lane, row = node & 127, node >> 7
        for c in range(3):
            found = corners[c * 8 : c * 8 + 8, here]
            for half in range(2):
                value = lookup(ghost[c, half : half + 1], lane)
                found = jnp.where(row == first + half, value, found)
            work[c * 8 : c * 8 + 8, here] = found
        work[24:32, here] = jnp.zeros((8, 128), jnp.float32)
        return carry

    lax.fori_loop(0, blocks, add_shared, 0, unroll=2)
    table = strain[...].astype(jnp.bfloat16)
    rate[...] = STEP_BRAIN * sum(
        jnp.dot(table, part, preferred_element_type=jnp.float32) for part in in_parts(work[...], 3)
    )

    def put(index, value):
        gains[index * 8 : index * 8 + 8, :] = jnp.broadcast_to(value, (8, 128))

    for r in range(regions):
        put(terms * regions + r, 2.0 * shear[r])
        put((terms + 1) * regions + r, bulk[r])
    for t in range(terms):
        span = jnp.full((8, 128), tau[t], jnp.float32)
        decay = jnp.exp(-STEP_BRAIN / span)
        put((terms + 2) * regions + t, decay)
        factor = (1.0 - decay) * span / STEP_BRAIN
        for r in range(regions):
            put(t * regions + r, (2.0 * shear[r] * weight[r, t]) * factor)

    def gain(index):
        return gains[index * 8 : index * 8 + 6, :]

    normal = lax.broadcasted_iota(jnp.int32, (6, 128), 0) < 3

    def block(b, carry):
        here = pl.ds(pl.multiple_of(b * 128, 128), 128)
        strains = rate[0:6, here]
        trace = rate[0:1, here] + rate[1:2, here] + rate[2:3, here]
        dev = jnp.where(normal, strains - trace / 3.0, 0.5 * strains)
        label = jnp.broadcast_to(region[:, here], (6, 128))
        masks = [label == r for r in range(regions)]

        def pick(t):
            chosen = jnp.zeros((6, 128), jnp.float32)
            for r, mask in enumerate(masks):
                chosen = jnp.where(mask, gain(t * regions + r), chosen)
            return chosen

        stress = pick(terms) * dev + jnp.where(normal, pick(terms + 1) * trace, 0.0)
        ready = []
        for t in range(terms):
            new = gain((terms + 2) * regions + t) * memory_in[t, :, here] + pick(t) * dev
            ready.append(new)
            stress = stress + new
        for t in range(terms):
            memory[t, :, here] = ready[t]
        rate[0:6, here] = jnp.where(label < regions, stress, 0.0)
        return carry

    lax.fori_loop(0, blocks, block, 0, unroll=2)
    rate[6:16, :] = jnp.zeros((10, elems), jnp.float32)
    table = spread[...].astype(jnp.bfloat16)
    work[...] = sum(jnp.dot(table, part, preferred_element_type=jnp.float32) for part in in_parts(rate[...], 2))

    low_rows = lax.broadcasted_iota(jnp.int32, (LO, elems), 0)
    high_rows = lax.broadcasted_iota(jnp.int32, (HI, elems), 0)

    def corner(q, sums):
        node = conn[pl.ds(q, 1), :]
        low = (low_rows == (node & (LO - 1))).astype(jnp.float32).astype(jnp.bfloat16)
        mine = high_rows == (node >> 7)
        parts = []
        for c in range(3):
            parts += in_parts(jnp.where(mine, work[pl.ds(c * 8 + q, 1), :], 0.0), 2)
        return sums + lax.dot_general(
            jnp.concatenate(parts, 0), low, (((1,), (1,)), ((), ())), preferred_element_type=jnp.float32
        )

    sums = lax.fori_loop(0, 8, corner, jnp.zeros((6 * HI, LO), jnp.float32))
    for c in range(3):
        at = c * 2 * HI
        whole = sums[at : at + HI] + sums[at + HI : at + 2 * HI]
        for h in range(first):
            here = slice(h * LO, h * LO + LO)
            old = vel[c : c + 1, here]
            kept = 1.0 if h < first - SHARED // LO else 1.0 - COUPLING
            base[c : c + 1, here] = kept * old + STEP_BRAIN * whole[h : h + 1] / mass[:, here]
        for half in range(SHARED // LO):
            shared[c : c + 1, half * LO : half * LO + LO] = whole[first + half : first + half + 1]
    scale[...] = STEP_BRAIN / mass[:, 0:SHARED]


def finish_kernel(sent, got_a, got_b, base, scale, place, share, out):
    nodes = base.shape[1]
    tables = sent.shape[1] - 2
    lane, row = place[...] & 127, place[...] >> 7
    for c in range(3):
        before = from_previous(got_b[c], got_a[c])
        after = from_next(got_b[c], got_a[c])
        found = jnp.zeros((8, 128), jnp.float32)
        for slot, values in enumerate((before, sent[c], after)):
            for r in range(tables):
                found = jnp.where(row == slot * tables + r, lookup(values[r : r + 1], lane), found)
        found = found * share[...]
        target = jnp.concatenate(
            [jnp.sum(found[0:4], 0, keepdims=True), jnp.sum(found[4:8], 0, keepdims=True)], 1
        )
        incoming = jnp.concatenate([before[tables : tables + 1], before[tables + 1 : tables + 2]], 1)
        split = nodes - SHARED
        out[c : c + 1, 0:SHARED] = base[c : c + 1, 0:SHARED] + incoming * scale[...]
        out[c : c + 1, SHARED:split] = base[c : c + 1, SHARED:split]
        out[c : c + 1, split:] = base[c : c + 1, split:] + COUPLING * target


def on_device(
    skull_state, stiffness, intersection_src, intersection_weight, brain_vel, connectivity, region,
    shear_table, bulk_table, prony_weight, prony_tau, prony_state, node_mass,
):
    lanes = skull_state.shape[2]
    columns = lanes // 128
    nodes = brain_vel.shape[1]
    elems = connectivity.shape[1]
    terms, regions = prony_weight.shape
    count = lax.axis_size("slab")
    vmem = pl.BlockSpec(memory_space=pltpu.VMEM)
    smem = pl.BlockSpec(memory_space=pltpu.SMEM)
    hbm = pl.BlockSpec(memory_space=pltpu.HBM)
    shape = lambda *dims: jax.ShapeDtypeStruct(dims, jnp.float32)
    scratch = lambda *dims: pltpu.VMEM(dims, jnp.float32)

    def kernel(body, out, operands, results, scratch_shapes=(), flops=1_000_000, vmem_mib=32):
        return pl.pallas_call(
            body,
            out_shape=out,
            in_specs=operands,
            out_specs=results,
            scratch_shapes=list(scratch_shapes),
            compiler_params=pltpu.CompilerParams(vmem_limit_bytes=vmem_mib << 20),
            cost_estimate=pl.CostEstimate(flops=flops, bytes_accessed=4_000_000, transcendentals=0),
            name=body.__name__.removesuffix("_kernel"),
        )

    swap_a = [(i, i ^ 1) for i in range(count)]
    swap_b = [(i, ((i + 1) ^ 1) - 1) for i in range(1, count - 1)]

    def swap(value):
        return lax.ppermute(value, "slab", swap_b), lax.ppermute(value, "slab", swap_a)

    field = [scratch(3 * (columns + 2) * DEEP, 128), scratch(3 * columns * DEEP, 128)]
    slabs = field + field + [scratch(columns * DEEP, 128)]
    table = strain_rows()

    package = kernel(
        pack_kernel, shape(7, 8, lanes + EDGE), [hbm, hbm, hbm], hbm,
        [scratch(3, SHARED), scratch(7, 8, lanes + EDGE), pltpu.SemaphoreType.DMA((15,))], vmem_mib=60,
    )(skull_state, stiffness, brain_vel)
    got_b, got_a = swap(package)
    corners, place, share = kernel(
        corners_kernel,
        (shape(32, elems), jax.ShapeDtypeStruct((8, 128), jnp.int32), shape(8, 128)),
        [vmem] * 4,
        [vmem] * 3,
    )(brain_vel, connectivity, intersection_src.T, intersection_weight.T)
    memory, base, shared, scale = kernel(
        hexes_kernel,
        (shape(*prony_state.shape), shape(3, nodes), shape(3, SHARED), shape(1, SHARED)),
        [vmem] * 9 + [smem] * 4 + [vmem],
        [vmem] * 4,
        [scratch(32, elems), scratch(16, elems), scratch(((terms + 2) * regions + terms) * 8, 128)],
    )(
        got_a, got_b, corners, connectivity, region.reshape(1, elems), jnp.asarray(table), jnp.asarray(-table.T),
        brain_vel, node_mass.reshape(1, nodes), shear_table, bulk_table, prony_weight.T, prony_tau, prony_state,
    )
    skull_out, sent = kernel(
        skull_kernel,
        (shape(*skull_state.shape), shape(3, columns + 2, 128)),
        [vmem] * 5,
        [vmem] * 2,
        slabs,
    )(skull_state, stiffness, got_a, got_b, shared)
    back_b, back_a = swap(sent)
    brain_out = kernel(finish_kernel, shape(3, nodes), [vmem] * 7, vmem)(
        sent, back_a, back_b, base, scale, place, share
    )
    return skull_out, brain_out, memory


def solution(mesh):
    placed = (
        P(None, "slab", None),
        P("slab", None),
        P("slab", None),
        P("slab", None),
        P(None, "slab"),
        P(None, "slab"),
        P("slab"),
        P(),
        P(),
        P(),
        P(),
        P(None, None, "slab"),
        P("slab"),
    )
    return jax.shard_map(
        on_device,
        mesh=mesh,
        in_specs=placed,
        out_specs=(P(None, "slab", None), P(None, "slab"), P(None, None, "slab")),
        check_vma=False,
    )
```

```python
import jax
import jax.numpy as jnp
from jax import lax
from jax.experimental import pallas as pl
from jax.experimental.pallas import tpu as pltpu
from jax.sharding import PartitionSpec as P

SUBSTEPS = 8
SHARED = 256
STEP_BRAIN = 0.2
DAMPING = 0.05
COUPLING = 0.5
EDGE = 128
DEEP = 24
GROUP = 8
LO = 128
HI = 32


def lookup(row, lane):
    return jnp.take_along_axis(
        jnp.broadcast_to(row, lane.shape), lane, axis=1, mode="promise_in_bounds"
    )


def pack_kernel(state, stiff, vel, out, nodes, package, sems):
    lanes = state.shape[2]
    first = pltpu.make_async_copy(vel.at[:, 0:SHARED], nodes, sems.at[14])
    arrive = [
        pltpu.make_async_copy(state.at[c] if c < 6 else stiff, package.at[c, :, 0:lanes], sems.at[c]) for c in range(7)
    ]
    leave = [pltpu.make_async_copy(package.at[c], out.at[c], sems.at[7 + c]) for c in range(7)]
    first.start()
    for copy in arrive:
        copy.start()
    package[:, :, lanes:] = jnp.zeros((7, 8, EDGE), jnp.float32)
    first.wait()
    for c in range(3):
        for half in range(2):
            package[c, half : half + 1, lanes:] = nodes[c : c + 1, half * 128 : half * 128 + 128]
    for c in range(7):
        arrive[c].wait()
        leave[c].start()
    for copy in leave:
        copy.wait()


def is_odd():
    return lax.rem(lax.axis_index("slab"), 2) == 1


def from_previous(by_b, by_a):
    return jnp.where(is_odd(), by_a, by_b)


def from_next(by_b, by_a):
    return jnp.where(is_odd(), by_b, by_a)


def fill(d, v, k, state, stiff, got_a, got_b):
    columns = state.shape[2] // 128

    def column(j, carry):
        here = pl.ds(pl.multiple_of(j * 128, 128), 128)
        for c in range(7):
            own = state[c, :, here] if c < 6 else stiff[:, here]
            b, a = got_b[c, :, here], got_a[c, :, here]
            for slab, value in enumerate((from_previous(b, a), own, from_next(b, a))):
                at = slab * 8
                if c < 3:
                    d[pl.ds(pl.multiple_of((c * (columns + 2) + 1 + j) * DEEP + at, 8), 8), :] = value
                elif c < 6:
                    v[pl.ds(pl.multiple_of(((c - 3) * columns + j) * DEEP + at, 8), 8), :] = value
                else:
                    k[pl.ds(pl.multiple_of(j * DEEP + at, 8), 8), :] = value
        return carry

    lax.fori_loop(0, columns, column, 0, unroll=2)
    wrap(d, columns)


def wrap(d, columns):
    for c in range(3):
        base = c * (columns + 2) * DEEP
        d[base : base + DEEP, :] = d[base + columns * DEEP : base + (columns + 1) * DEEP, :]
        end = base + (columns + 1) * DEEP
        d[end : end + DEEP, :] = d[base + DEEP : base + 2 * DEEP, :]


def advance(d, v, k, windows, columns, emit):
    lane = lax.broadcasted_iota(jnp.int32, (8, 128), 1)
    first, last = lane == 0, lane == 127

    def group(g, carry):
        def at(ref, column, row):
            start = pl.multiple_of(g * (GROUP * DEEP), 8) + (column * DEEP + row)
            return ref[pl.ds(start, 8), :]

        for w in windows:
            stiffs = [at(k, i, w) for i in range(GROUP)]
            ready = []
            for c in range(3):
                base = c * (columns + 2)
                middles = [at(d, base + i, w) for i in range(GROUP + 2)]
                ahead = [pltpu.roll(m, 1, 1) for m in middles[:-1]]
                behind = [pltpu.roll(m, 127, 1) for m in middles[1:]]
                for i in range(GROUP):
                    left = jnp.where(first, ahead[i], ahead[i + 1])
                    right = jnp.where(last, behind[i + 1], behind[i])
                    middle = middles[i + 1]
                    above = at(d, base + i + 1, w - 1)
                    below = at(d, base + i + 1, w + 1)
                    laplace = (below + above) + (left + right) - 4.0 * middle
                    old = at(v, c * columns + i, w)
                    new = old + (stiffs[i] * laplace - DAMPING * old)
                    ready.append((w, c, g, i, middle + new, new))
            for item in ready:
                emit(*item)
        return carry

    lax.fori_loop(0, columns // GROUP, group, 0)


def keep(d, v, columns):
    def emit(w, c, g, i, new_d, new_v):
        base = pl.multiple_of(g * (GROUP * DEEP), 8)
        d[pl.ds(base + ((c * (columns + 2) + 1 + i) * DEEP + w), 8), :] = new_d
        v[pl.ds(base + ((c * columns + i) * DEEP + w), 8), :] = new_v

    return emit


WHOLE = [[1, 9, 15], [2, 10, 14], [3, 11, 13], [4, 12], [5, 11], [6, 10], [7, 9], [8]]


def skull_kernel(state, stiff, got_a, got_b, shared, out, send, d0, v0, d1, v1, k):
    columns = state.shape[2] // 128
    fill(d0, v0, k, state, stiff, got_a, got_b)
    now, later = (d0, v0), (d1, v1)
    for c in range(3):
        for half in range(2):
            send[c, columns + half : columns + half + 1, :] = shared[c : c + 1, half * 128 : half * 128 + 128]

    def last(w, c, g, i, new_d, new_v):
        here = pl.ds(pl.multiple_of(g * (GROUP * 128), 128) + i * 128, 128)
        out[c, :, here] = new_d
        out[3 + c, :, here] = new_v
        base = pl.multiple_of(g * (GROUP * DEEP), 8)
        v0[pl.ds(base + ((c * columns + i) * DEEP + w), 8), :] = new_v

    for step in range(SUBSTEPS):
        ends = step == SUBSTEPS - 1
        advance(*now, k, WHOLE[step], columns, last if ends else keep(*later, columns))
        if not ends:
            wrap(later[0], columns)
        now, later = later, now
        for c in range(3):
            row = now[1][pl.ds(c * columns * DEEP + 15, columns, stride=DEEP), :]
            part = ((step + 1.0) / 36.0) * row
            send[c, 0:columns, :] = part if step == 0 else send[c, 0:columns, :] + part


def prepare_kernel(vel, conn, src, weight, shear, bulk, prony, tau, corners, nodes, place, share, gains):
    regions, terms = prony.shape
    blocks = conn.shape[1] // 128
    tables = vel.shape[1] // 128
    normed = weight[...] / jnp.sum(weight[...], 0, keepdims=True)
    for half in range(2):
        place[half * 4 : half * 4 + 4, :] = src[:, half * 128 : half * 128 + 128]
        share[half * 4 : half * 4 + 4, :] = normed[:, half * 128 : half * 128 + 128]

    def put(index, value):
        gains[index * 8 : index * 8 + 8, :] = jnp.broadcast_to(value, (8, 128))

    for r in range(regions):
        put(terms * regions + r, 2.0 * shear[r])
        put((terms + 1) * regions + r, bulk[r])
    for t in range(terms):
        span = jnp.full((8, 128), tau[t], jnp.float32)
        decay = jnp.exp(-STEP_BRAIN / span)
        put((terms + 2) * regions + t, decay)
        factor = (1.0 - decay) * span / STEP_BRAIN
        for r in range(regions):
            put(t * regions + r, (2.0 * shear[r] * prony[r, t]) * factor)
    for b in range(blocks):
        nodes[pl.ds(b, 8, stride=blocks), :] = conn[:, b * 128 : b * 128 + 128]

    def block(i, carry):
        here = pl.ds(pl.multiple_of(i * 8, 8), 8)
        node = nodes[here, :]
        lane, row = node & 127, node >> 7
        found = [jnp.zeros((8, 128), jnp.float32) for _ in range(3)]
        for r in range(tables):
            mine = row == r
            for c in range(3):
                value = lookup(vel[c : c + 1, r * 128 : r * 128 + 128], lane)
                found[c] = jnp.where(mine, value, found[c])
        for c in range(3):
            corners[pl.ds(pl.multiple_of(c * 8 * blocks + i * 8, 8), 8), :] = found[c]
        return carry

    lax.fori_loop(0, blocks, block, 0)


def in_parts(value, count):
    parts = []
    for _ in range(count):
        part = value.astype(jnp.bfloat16)
        value = value - part.astype(jnp.float32)
        parts.append(part)
    return parts


def hexes_kernel(
    got_a, got_b, corners, nodes, region, vel, mass, memory_in, gains,
    memory, base, shared, scale,
    work, rate,
):
    elems = memory_in.shape[2]
    terms = memory_in.shape[0]
    regions = (gains.shape[0] // 8 - terms) // (terms + 2)
    blocks = elems // 128
    lanes = got_b.shape[2] - EDGE
    ghost = from_next(got_b[0:3, :, lanes:], got_a[0:3, :, lanes:])
    first = base.shape[1] // 128

    def add_shared(i, carry):
        node = nodes[pl.ds(pl.multiple_of(i * 8, 8), 8), :]
        lane, row = node & 127, node >> 7
        for c in range(3):
            here = pl.ds(pl.multiple_of(c * 8 * blocks + i * 8, 8), 8)
            found = corners[here, :]
            for half in range(2):
                found = jnp.where(row == first + half, lookup(ghost[c, half : half + 1], lane), found)
            work[here, :] = found
        return carry

    lax.fori_loop(0, blocks, add_shared, 0, unroll=4)

    def dense(c, q):
        return slice((c * 8 + q) * blocks, (c * 8 + q + 1) * blocks)

    slopes = []
    for c in range(3):
        v = [(0.25 * STEP_BRAIN) * work[dense(c, q), :] for q in range(8)]
        low = [v[q] + v[q + 1] for q in range(0, 8, 2)]
        along = [v[q + 1] - v[q] for q in range(0, 8, 2)]
        slopes.append(
            [
                (along[0] + along[1]) + (along[2] + along[3]),
                (low[1] - low[0]) + (low[3] - low[2]),
                (low[2] + low[3]) - (low[0] + low[1]),
            ]
        )
    strains = [slopes[c][c] for c in range(3)]
    trace = strains[0] + strains[1] + strains[2]
    devs = [strain - trace / 3.0 for strain in strains]
    devs += [0.5 * (slopes[a][b] + slopes[b][a]) for a, b in ((0, 1), (1, 2), (0, 2))]
    for i, value in enumerate(devs + [trace]):
        rate[pl.ds(i, blocks, stride=8), :] = value

    def gain(index):
        return gains[index * 8 : index * 8 + 6, :]

    normal = lax.broadcasted_iota(jnp.int32, (6, 128), 0) < 3

    def block(b, carry):
        here = pl.ds(pl.multiple_of(b * 128, 128), 128)
        mine = pl.multiple_of(b * 8, 8)
        dev = rate[pl.ds(mine, 6), :]
        trace = rate[pl.ds(mine + 6, 1), :]
        label = jnp.broadcast_to(region[:, here], (6, 128))
        masks = [label == r for r in range(regions)]

        def pick(t):
            chosen = jnp.zeros((6, 128), jnp.float32)
            for r, mask in enumerate(masks):
                chosen = jnp.where(mask, gain(t * regions + r), chosen)
            return chosen

        stress = pick(terms) * dev + jnp.where(normal, pick(terms + 1) * trace, 0.0)
        ready = []
        for t in range(terms):
            new = gain((terms + 2) * regions + t) * memory_in[t, :, here] + pick(t) * dev
            ready.append(new)
            stress = stress + new
        for t in range(terms):
            memory[t, :, here] = ready[t]
        rate[pl.ds(mine, 6), :] = jnp.where(label < regions, stress, 0.0)
        return carry

    lax.fori_loop(0, blocks, block, 0, unroll=2)
    stress = [0.25 * rate[pl.ds(i, blocks, stride=8), :] for i in range(6)]
    for c, (a, b, d) in enumerate(((0, 3, 5), (3, 1, 4), (5, 4, 2))):
        plus, minus = stress[a] + stress[b], stress[a] - stress[b]
        for q, value in ((7, plus + stress[d]), (3, plus - stress[d]), (5, minus + stress[d]), (1, minus - stress[d])):
            work[dense(c, q), :] = -value
            work[dense(c, 7 - q), :] = value

    low_rows = lax.broadcasted_iota(jnp.int32, (LO, 128), 0)
    high_rows = lax.broadcasted_iota(jnp.int32, (HI, 128), 0)

    def corner(q, sums):
        lows, parts = [], [[] for _ in range(6)]
        for b in range(blocks):
            node = nodes[pl.ds(q * blocks + b, 1), :]
            lows.append((low_rows == (node & (LO - 1))).astype(jnp.float32).astype(jnp.bfloat16))
            mine = high_rows == (node >> 7)
            for c in range(3):
                force = jnp.where(mine, work[pl.ds((c * 8 + q) * blocks + b, 1), :], 0.0)
                for p, part in enumerate(in_parts(force, 2)):
                    parts[c * 2 + p].append(part)
        left = jnp.concatenate([jnp.concatenate(row, 1) for row in parts], 0)
        return sums + lax.dot_general(
            left, jnp.concatenate(lows, 1), (((1,), (1,)), ((), ())), preferred_element_type=jnp.float32
        )

    sums = lax.fori_loop(0, 8, corner, jnp.zeros((6 * HI, LO), jnp.float32), unroll=2)
    for c in range(3):
        at = c * 2 * HI
        whole = sums[at : at + HI] + sums[at + HI : at + 2 * HI]
        for h in range(first):
            here = slice(h * LO, h * LO + LO)
            old = vel[c : c + 1, here]
            kept = 1.0 if h < first - SHARED // LO else 1.0 - COUPLING
            base[c : c + 1, here] = kept * old + STEP_BRAIN * whole[h : h + 1] / mass[:, here]
        for half in range(SHARED // LO):
            shared[c : c + 1, half * LO : half * LO + LO] = whole[first + half : first + half + 1]
    scale[...] = STEP_BRAIN / mass[:, 0:SHARED]


def finish_kernel(sent, got_a, got_b, base, scale, place, share, out):
    nodes = base.shape[1]
    tables = sent.shape[1] - 2
    lane, row = place[...] & 127, place[...] >> 7
    for c in range(3):
        before = from_previous(got_b[c], got_a[c])
        after = from_next(got_b[c], got_a[c])
        found = jnp.zeros((8, 128), jnp.float32)
        for slot, values in enumerate((before, sent[c], after)):
            for r in range(tables):
                found = jnp.where(row == slot * tables + r, lookup(values[r : r + 1], lane), found)
        found = found * share[...]
        target = jnp.concatenate(
            [jnp.sum(found[0:4], 0, keepdims=True), jnp.sum(found[4:8], 0, keepdims=True)], 1
        )
        incoming = jnp.concatenate([before[tables : tables + 1], before[tables + 1 : tables + 2]], 1)
        split = nodes - SHARED
        out[c : c + 1, 0:SHARED] = base[c : c + 1, 0:SHARED] + incoming * scale[...]
        out[c : c + 1, SHARED:split] = base[c : c + 1, SHARED:split]
        out[c : c + 1, split:] = base[c : c + 1, split:] + COUPLING * target


def on_device(
    skull_state, stiffness, intersection_src, intersection_weight, brain_vel, connectivity, region,
    shear_table, bulk_table, prony_weight, prony_tau, prony_state, node_mass,
):
    lanes = skull_state.shape[2]
    columns = lanes // 128
    nodes = brain_vel.shape[1]
    elems = connectivity.shape[1]
    terms, regions = prony_weight.shape
    count = lax.axis_size("slab")
    vmem = pl.BlockSpec(memory_space=pltpu.VMEM)
    smem = pl.BlockSpec(memory_space=pltpu.SMEM)
    hbm = pl.BlockSpec(memory_space=pltpu.HBM)
    shape = lambda *dims: jax.ShapeDtypeStruct(dims, jnp.float32)
    scratch = lambda *dims: pltpu.VMEM(dims, jnp.float32)

    def kernel(body, out, operands, results, scratch_shapes=(), flops=1_000_000, vmem_mib=32):
        return pl.pallas_call(
            body,
            out_shape=out,
            in_specs=operands,
            out_specs=results,
            scratch_shapes=list(scratch_shapes),
            compiler_params=pltpu.CompilerParams(vmem_limit_bytes=vmem_mib << 20),
            cost_estimate=pl.CostEstimate(flops=flops, bytes_accessed=4_000_000, transcendentals=0),
            name=body.__name__.removesuffix("_kernel"),
        )

    swap_a = [(i, i ^ 1) for i in range(count)]
    swap_b = [(i, ((i + 1) ^ 1) - 1) for i in range(1, count - 1)]

    def swap(value):
        return lax.ppermute(value, "slab", swap_b), lax.ppermute(value, "slab", swap_a)

    field = [scratch(3 * (columns + 2) * DEEP, 128), scratch(3 * columns * DEEP, 128)]
    slabs = field + field + [scratch(columns * DEEP, 128)]

    package = kernel(
        pack_kernel, shape(7, 8, lanes + EDGE), [hbm, hbm, hbm], hbm,
        [scratch(3, SHARED), scratch(7, 8, lanes + EDGE), pltpu.SemaphoreType.DMA((15,))], vmem_mib=60,
    )(skull_state, stiffness, brain_vel)
    got_b, got_a = swap(package)
    gain_rows = ((terms + 2) * regions + terms) * 8
    index = lambda *dims: jax.ShapeDtypeStruct(dims, jnp.int32)
    blocks = elems // 128
    corners, dense_nodes, place, share, gains = kernel(
        prepare_kernel,
        (shape(24 * blocks, 128), index(8 * blocks, 128), index(8, 128), shape(8, 128), shape(gain_rows, 128)),
        [vmem] * 4 + [smem] * 4,
        [vmem] * 5,
    )(
        brain_vel, connectivity, intersection_src.T, intersection_weight.T,
        shear_table, bulk_table, prony_weight.T, prony_tau,
    )
    memory, base, shared, scale = kernel(
        hexes_kernel,
        (shape(*prony_state.shape), shape(3, nodes), shape(3, SHARED), shape(1, SHARED)),
        [vmem] * 9,
        [vmem] * 4,
        [scratch(24 * blocks, 128), scratch(8 * blocks, 128)],
    )(
        got_a, got_b, corners, dense_nodes, region.reshape(1, elems),
        brain_vel, node_mass.reshape(1, nodes), prony_state, gains,
    )
    skull_out, sent = kernel(
        skull_kernel,
        (shape(*skull_state.shape), shape(3, columns + 2, 128)),
        [vmem] * 5,
        [vmem] * 2,
        slabs,
    )(skull_state, stiffness, got_a, got_b, shared)
    back_b, back_a = swap(sent)
    brain_out = kernel(finish_kernel, shape(3, nodes), [vmem] * 7, vmem)(
        sent, back_a, back_b, base, scale, place, share
    )
    return skull_out, brain_out, memory


def solution(mesh):
    placed = (
        P(None, "slab", None),
        P("slab", None),
        P("slab", None),
        P("slab", None),
        P(None, "slab"),
        P(None, "slab"),
        P("slab"),
        P(),
        P(),
        P(),
        P(),
        P(None, None, "slab"),
        P("slab"),
    )
    return jax.shard_map(
        on_device,
        mesh=mesh,
        in_specs=placed,
        out_specs=(P(None, "slab", None), P(None, "slab"), P(None, None, "slab")),
        check_vma=False,
    )
```

```python
import jax
import jax.numpy as jnp
from jax import lax
from jax.experimental import pallas as pl
from jax.experimental.pallas import tpu as pltpu
from jax.sharding import PartitionSpec as P

SUBSTEPS = 8
SHARED = 256
STEP_BRAIN = 0.2
DAMPING = 0.05
COUPLING = 0.5
EDGE = 128
DEEP = 24
GROUP = 8
LO = 128
HI = 32


def lookup(row, lane):
    return jnp.take_along_axis(
        jnp.broadcast_to(row, lane.shape), lane, axis=1, mode="promise_in_bounds"
    )


def pack_kernel(state, stiff, vel, out, nodes, package, sems):
    lanes = state.shape[2]
    first = pltpu.make_async_copy(vel.at[:, 0:SHARED], nodes, sems.at[14])
    arrive = [
        pltpu.make_async_copy(state.at[c] if c < 6 else stiff, package.at[c, :, 0:lanes], sems.at[c]) for c in range(7)
    ]
    leave = [pltpu.make_async_copy(package.at[c], out.at[c], sems.at[7 + c]) for c in range(7)]
    first.start()
    for copy in arrive:
        copy.start()
    package[:, :, lanes:] = jnp.zeros((7, 8, EDGE), jnp.float32)
    first.wait()
    for c in range(3):
        for half in range(2):
            package[c, half : half + 1, lanes:] = nodes[c : c + 1, half * 128 : half * 128 + 128]
    for c in range(7):
        arrive[c].wait()
        leave[c].start()
    for copy in leave:
        copy.wait()


def is_odd():
    return lax.rem(lax.axis_index("slab"), 2) == 1


def from_previous(by_b, by_a):
    return jnp.where(is_odd(), by_a, by_b)


def from_next(by_b, by_a):
    return jnp.where(is_odd(), by_b, by_a)


def fill(d, v, k, state, stiff, got_a, got_b):
    columns = state.shape[2] // 128

    def column(j, carry):
        here = pl.ds(pl.multiple_of(j * 128, 128), 128)
        values = []
        for c in range(7):
            own = state[c, :, here] if c < 6 else stiff[:, here]
            b, a = got_b[c, :, here], got_a[c, :, here]
            values.append((from_previous(b, a), own, from_next(b, a)))
        for c in range(7):
            for slab, value in enumerate(values[c]):
                at = slab * 8
                if c < 3:
                    d[pl.ds(pl.multiple_of((c * (columns + 2) + 1 + j) * DEEP + at, 8), 8), :] = value
                elif c < 6:
                    v[pl.ds(pl.multiple_of(((c - 3) * columns + j) * DEEP + at, 8), 8), :] = value
                else:
                    k[pl.ds(pl.multiple_of(j * DEEP + at, 8), 8), :] = value
        return carry

    lax.fori_loop(0, columns, column, 0, unroll=2)
    wrap(d, columns)


def wrap(d, columns):
    for c in range(3):
        base = c * (columns + 2) * DEEP
        d[base : base + DEEP, :] = d[base + columns * DEEP : base + (columns + 1) * DEEP, :]
        end = base + (columns + 1) * DEEP
        d[end : end + DEEP, :] = d[base + DEEP : base + 2 * DEEP, :]


def advance(d, v, k, windows, columns, emit):
    lane = lax.broadcasted_iota(jnp.int32, (8, 128), 1)
    first, last = lane == 0, lane == 127

    def group(g, carry):
        def at(ref, column, row):
            start = pl.multiple_of(g * (GROUP * DEEP), 8) + (column * DEEP + row)
            return ref[pl.ds(start, 8), :]

        ready = []
        for w in windows:
            stiffs = [at(k, i, w) for i in range(GROUP)]
            for c in range(3):
                base = c * (columns + 2)
                middles = [at(d, base + i, w) for i in range(GROUP + 2)]
                ahead = [pltpu.roll(m, 1, 1) for m in middles[:-1]]
                behind = [pltpu.roll(m, 127, 1) for m in middles[1:]]
                for i in range(GROUP):
                    left = jnp.where(first, ahead[i], ahead[i + 1])
                    right = jnp.where(last, behind[i + 1], behind[i])
                    middle = middles[i + 1]
                    above = at(d, base + i + 1, w - 1)
                    below = at(d, base + i + 1, w + 1)
                    laplace = (below + above) + (left + right) - 4.0 * middle
                    old = at(v, c * columns + i, w)
                    new = old + (stiffs[i] * laplace - DAMPING * old)
                    ready.append((w, c, g, i, middle + new, new))
        for item in ready:
            emit(*item)
        return carry

    lax.fori_loop(0, columns // GROUP, group, 0)


def keep(d, v, columns):
    def emit(w, c, g, i, new_d, new_v):
        base = pl.multiple_of(g * (GROUP * DEEP), 8)
        d[pl.ds(base + ((c * (columns + 2) + 1 + i) * DEEP + w), 8), :] = new_d
        v[pl.ds(base + ((c * columns + i) * DEEP + w), 8), :] = new_v

    return emit


WHOLE = [[1, 9, 15], [2, 10, 14], [3, 11, 13], [4, 12], [5, 11], [6, 10], [7, 9], [8]]


def skull_kernel(state, stiff, got_a, got_b, shared, out, send, d0, v0, d1, v1, k):
    columns = state.shape[2] // 128
    fill(d0, v0, k, state, stiff, got_a, got_b)
    now, later = (d0, v0), (d1, v1)
    for c in range(3):
        for half in range(2):
            send[c, columns + half : columns + half + 1, :] = shared[c : c + 1, half * 128 : half * 128 + 128]

    def last(w, c, g, i, new_d, new_v):
        here = pl.ds(pl.multiple_of(g * (GROUP * 128), 128) + i * 128, 128)
        out[c, :, here] = new_d
        out[3 + c, :, here] = new_v
        base = pl.multiple_of(g * (GROUP * DEEP), 8)
        v0[pl.ds(base + ((c * columns + i) * DEEP + w), 8), :] = new_v

    for step in range(SUBSTEPS):
        ends = step == SUBSTEPS - 1
        advance(*now, k, WHOLE[step], columns, last if ends else keep(*later, columns))
        if not ends:
            wrap(later[0], columns)
        now, later = later, now
        for c in range(3):
            row = now[1][pl.ds(c * columns * DEEP + 15, columns, stride=DEEP), :]
            part = ((step + 1.0) / 36.0) * row
            send[c, 0:columns, :] = part if step == 0 else send[c, 0:columns, :] + part


def prepare_kernel(vel, conn, src, weight, shear, bulk, prony, tau, corners, nodes, place, share, gains):
    regions, terms = prony.shape
    blocks = conn.shape[1] // 128
    tables = vel.shape[1] // 128
    normed = weight[...] / jnp.sum(weight[...], 0, keepdims=True)
    for half in range(2):
        place[half * 4 : half * 4 + 4, :] = src[:, half * 128 : half * 128 + 128]
        share[half * 4 : half * 4 + 4, :] = normed[:, half * 128 : half * 128 + 128]

    def put(index, value):
        gains[index * 8 : index * 8 + 8, :] = jnp.broadcast_to(value, (8, 128))

    for r in range(regions):
        put(terms * regions + r, 2.0 * shear[r])
        put((terms + 1) * regions + r, bulk[r])
    for t in range(terms):
        span = jnp.full((8, 128), tau[t], jnp.float32)
        decay = jnp.exp(-STEP_BRAIN / span)
        put((terms + 2) * regions + t, decay)
        factor = (1.0 - decay) * span / STEP_BRAIN
        for r in range(regions):
            put(t * regions + r, (2.0 * shear[r] * prony[r, t]) * factor)
    for b in range(blocks):
        nodes[pl.ds(b, 8, stride=blocks), :] = conn[:, b * 128 : b * 128 + 128]

    def block(i, carry):
        here = pl.ds(pl.multiple_of(i * 8, 8), 8)
        node = nodes[here, :]
        lane, row = node & 127, node >> 7
        found = [jnp.zeros((8, 128), jnp.float32) for _ in range(3)]
        for r in range(tables):
            mine = row == r
            for c in range(3):
                value = lookup(vel[c : c + 1, r * 128 : r * 128 + 128], lane)
                found[c] = jnp.where(mine, value, found[c])
        for c in range(3):
            corners[pl.ds(pl.multiple_of(c * 8 * blocks + i * 8, 8), 8), :] = found[c]
        return carry

    lax.fori_loop(0, blocks, block, 0)


def in_parts(value, count):
    parts = []
    for _ in range(count):
        part = value.astype(jnp.bfloat16)
        value = value - part.astype(jnp.float32)
        parts.append(part)
    return parts


def hexes_kernel(
    got_a, got_b, corners, nodes, region, vel, mass, memory_in, gains,
    memory, base, shared, scale,
    work, rate,
):
    elems = memory_in.shape[2]
    terms = memory_in.shape[0]
    regions = (gains.shape[0] // 8 - terms) // (terms + 2)
    blocks = elems // 128
    lanes = got_b.shape[2] - EDGE
    ghost = from_next(got_b[0:3, :, lanes:], got_a[0:3, :, lanes:])
    first = base.shape[1] // 128

    def add_shared(i, carry):
        node = nodes[pl.ds(pl.multiple_of(i * 8, 8), 8), :]
        lane, row = node & 127, node >> 7
        for c in range(3):
            here = pl.ds(pl.multiple_of(c * 8 * blocks + i * 8, 8), 8)
            found = corners[here, :]
            for half in range(2):
                found = jnp.where(row == first + half, lookup(ghost[c, half : half + 1], lane), found)
            work[here, :] = found
        return carry

    lax.fori_loop(0, blocks, add_shared, 0, unroll=4)

    def dense(c, q):
        return slice((c * 8 + q) * blocks, (c * 8 + q + 1) * blocks)

    slopes = []
    for c in range(3):
        v = [(0.25 * STEP_BRAIN) * work[dense(c, q), :] for q in range(8)]
        low = [v[q] + v[q + 1] for q in range(0, 8, 2)]
        along = [v[q + 1] - v[q] for q in range(0, 8, 2)]
        slopes.append(
            [
                (along[0] + along[1]) + (along[2] + along[3]),
                (low[1] - low[0]) + (low[3] - low[2]),
                (low[2] + low[3]) - (low[0] + low[1]),
            ]
        )
    strains = [slopes[c][c] for c in range(3)]
    trace = strains[0] + strains[1] + strains[2]
    devs = [strain - trace / 3.0 for strain in strains]
    devs += [0.5 * (slopes[a][b] + slopes[b][a]) for a, b in ((0, 1), (1, 2), (0, 2))]
    for i, value in enumerate(devs + [trace]):
        rate[pl.ds(i, blocks, stride=8), :] = value

    def gain(index):
        return gains[index * 8 : index * 8 + 6, :]

    normal = lax.broadcasted_iota(jnp.int32, (6, 128), 0) < 3

    def block(b, carry):
        here = pl.ds(pl.multiple_of(b * 128, 128), 128)
        mine = pl.multiple_of(b * 8, 8)
        dev = rate[pl.ds(mine, 6), :]
        trace = rate[pl.ds(mine + 6, 1), :]
        label = jnp.broadcast_to(region[:, here], (6, 128))
        masks = [label == r for r in range(regions)]

        def pick(t):
            chosen = jnp.zeros((6, 128), jnp.float32)
            for r, mask in enumerate(masks):
                chosen = jnp.where(mask, gain(t * regions + r), chosen)
            return chosen

        stress = pick(terms) * dev + jnp.where(normal, pick(terms + 1) * trace, 0.0)
        ready = []
        for t in range(terms):
            new = gain((terms + 2) * regions + t) * memory_in[t, :, here] + pick(t) * dev
            ready.append(new)
            stress = stress + new
        for t in range(terms):
            memory[t, :, here] = ready[t]
        rate[pl.ds(mine, 6), :] = jnp.where(label < regions, stress, 0.0)
        return carry

    lax.fori_loop(0, blocks, block, 0, unroll=2)
    stress = [0.25 * rate[pl.ds(i, blocks, stride=8), :] for i in range(6)]
    for c, (a, b, d) in enumerate(((0, 3, 5), (3, 1, 4), (5, 4, 2))):
        plus, minus = stress[a] + stress[b], stress[a] - stress[b]
        for q, value in ((7, plus + stress[d]), (3, plus - stress[d]), (5, minus + stress[d]), (1, minus - stress[d])):
            work[dense(c, q), :] = -value
            work[dense(c, 7 - q), :] = value

    low_rows = lax.broadcasted_iota(jnp.int32, (LO, 128), 0)
    high_rows = lax.broadcasted_iota(jnp.int32, (HI, 128), 0)

    def corner(q, sums):
        lows, parts = [], [[] for _ in range(6)]
        for b in range(blocks):
            node = nodes[pl.ds(q * blocks + b, 1), :]
            lows.append((low_rows == (node & (LO - 1))).astype(jnp.float32).astype(jnp.bfloat16))
            mine = high_rows == (node >> 7)
            for c in range(3):
                force = jnp.where(mine, work[pl.ds((c * 8 + q) * blocks + b, 1), :], 0.0)
                for p, part in enumerate(in_parts(force, 2)):
                    parts[c * 2 + p].append(part)
        left = jnp.concatenate([jnp.concatenate(row, 1) for row in parts], 0)
        return sums + lax.dot_general(
            left, jnp.concatenate(lows, 1), (((1,), (1,)), ((), ())), preferred_element_type=jnp.float32
        )

    sums = lax.fori_loop(0, 8, corner, jnp.zeros((6 * HI, LO), jnp.float32), unroll=2)
    for c in range(3):
        at = c * 2 * HI
        whole = sums[at : at + HI] + sums[at + HI : at + 2 * HI]
        for h in range(first):
            here = slice(h * LO, h * LO + LO)
            old = vel[c : c + 1, here]
            kept = 1.0 if h < first - SHARED // LO else 1.0 - COUPLING
            base[c : c + 1, here] = kept * old + STEP_BRAIN * whole[h : h + 1] / mass[:, here]
        for half in range(SHARED // LO):
            shared[c : c + 1, half * LO : half * LO + LO] = whole[first + half : first + half + 1]
    scale[...] = STEP_BRAIN / mass[:, 0:SHARED]


def finish_kernel(sent, got_a, got_b, base, scale, place, share, out):
    nodes = base.shape[1]
    tables = sent.shape[1] - 2
    lane, row = place[...] & 127, place[...] >> 7
    for c in range(3):
        before = from_previous(got_b[c], got_a[c])
        after = from_next(got_b[c], got_a[c])
        found = jnp.zeros((8, 128), jnp.float32)
        for slot, values in enumerate((before, sent[c], after)):
            for r in range(tables):
                found = jnp.where(row == slot * tables + r, lookup(values[r : r + 1], lane), found)
        found = found * share[...]
        target = jnp.concatenate(
            [jnp.sum(found[0:4], 0, keepdims=True), jnp.sum(found[4:8], 0, keepdims=True)], 1
        )
        incoming = jnp.concatenate([before[tables : tables + 1], before[tables + 1 : tables + 2]], 1)
        split = nodes - SHARED
        out[c : c + 1, 0:SHARED] = base[c : c + 1, 0:SHARED] + incoming * scale[...]
        out[c : c + 1, SHARED:split] = base[c : c + 1, SHARED:split]
        out[c : c + 1, split:] = base[c : c + 1, split:] + COUPLING * target


def on_device(
    skull_state, stiffness, intersection_src, intersection_weight, brain_vel, connectivity, region,
    shear_table, bulk_table, prony_weight, prony_tau, prony_state, node_mass,
):
    lanes = skull_state.shape[2]
    columns = lanes // 128
    nodes = brain_vel.shape[1]
    elems = connectivity.shape[1]
    terms, regions = prony_weight.shape
    count = lax.axis_size("slab")
    vmem = pl.BlockSpec(memory_space=pltpu.VMEM)
    smem = pl.BlockSpec(memory_space=pltpu.SMEM)
    hbm = pl.BlockSpec(memory_space=pltpu.HBM)
    shape = lambda *dims: jax.ShapeDtypeStruct(dims, jnp.float32)
    scratch = lambda *dims: pltpu.VMEM(dims, jnp.float32)

    def kernel(body, out, operands, results, scratch_shapes=(), flops=1_000_000, vmem_mib=32):
        return pl.pallas_call(
            body,
            out_shape=out,
            in_specs=operands,
            out_specs=results,
            scratch_shapes=list(scratch_shapes),
            compiler_params=pltpu.CompilerParams(vmem_limit_bytes=vmem_mib << 20),
            cost_estimate=pl.CostEstimate(flops=flops, bytes_accessed=4_000_000, transcendentals=0),
            name=body.__name__.removesuffix("_kernel"),
        )

    swap_a = [(i, i ^ 1) for i in range(count)]
    swap_b = [(i, ((i + 1) ^ 1) - 1) for i in range(1, count - 1)]

    def swap(value):
        return lax.ppermute(value, "slab", swap_b), lax.ppermute(value, "slab", swap_a)

    field = [scratch(3 * (columns + 2) * DEEP, 128), scratch(3 * columns * DEEP, 128)]
    slabs = field + field + [scratch(columns * DEEP, 128)]

    package = kernel(
        pack_kernel, shape(7, 8, lanes + EDGE), [hbm, hbm, hbm], hbm,
        [scratch(3, SHARED), scratch(7, 8, lanes + EDGE), pltpu.SemaphoreType.DMA((15,))], vmem_mib=60,
    )(skull_state, stiffness, brain_vel)
    got_b, got_a = swap(package)
    gain_rows = ((terms + 2) * regions + terms) * 8
    index = lambda *dims: jax.ShapeDtypeStruct(dims, jnp.int32)
    blocks = elems // 128
    corners, dense_nodes, place, share, gains = kernel(
        prepare_kernel,
        (shape(24 * blocks, 128), index(8 * blocks, 128), index(8, 128), shape(8, 128), shape(gain_rows, 128)),
        [vmem] * 4 + [smem] * 4,
        [vmem] * 5,
    )(
        brain_vel, connectivity, intersection_src.T, intersection_weight.T,
        shear_table, bulk_table, prony_weight.T, prony_tau,
    )
    memory, base, shared, scale = kernel(
        hexes_kernel,
        (shape(*prony_state.shape), shape(3, nodes), shape(3, SHARED), shape(1, SHARED)),
        [vmem] * 9,
        [vmem] * 4,
        [scratch(24 * blocks, 128), scratch(8 * blocks, 128)],
    )(
        got_a, got_b, corners, dense_nodes, region.reshape(1, elems),
        brain_vel, node_mass.reshape(1, nodes), prony_state, gains,
    )
    skull_out, sent = kernel(
        skull_kernel,
        (shape(*skull_state.shape), shape(3, columns + 2, 128)),
        [vmem] * 5,
        [vmem] * 2,
        slabs,
    )(skull_state, stiffness, got_a, got_b, shared)
    back_b, back_a = swap(sent)
    brain_out = kernel(finish_kernel, shape(3, nodes), [vmem] * 7, vmem)(
        sent, back_a, back_b, base, scale, place, share
    )
    return skull_out, brain_out, memory


def solution(mesh):
    placed = (
        P(None, "slab", None),
        P("slab", None),
        P("slab", None),
        P("slab", None),
        P(None, "slab"),
        P(None, "slab"),
        P("slab"),
        P(),
        P(),
        P(),
        P(),
        P(None, None, "slab"),
        P("slab"),
    )
    return jax.shard_map(
        on_device,
        mesh=mesh,
        in_specs=placed,
        out_specs=(P(None, "slab", None), P(None, "slab"), P(None, None, "slab")),
        check_vma=False,
    )
```

```python
import jax
import jax.numpy as jnp
from jax import lax
from jax.experimental import pallas as pl
from jax.experimental.pallas import tpu as pltpu
from jax.sharding import PartitionSpec as P

SUBSTEPS = 8
SHARED = 256
STEP_BRAIN = 0.2
DAMPING = 0.05
COUPLING = 0.5
EDGE = 128
DEEP = 24
GROUP = 16
LO = 128
HI = 32


def lookup(row, lane):
    return jnp.take_along_axis(
        jnp.broadcast_to(row, lane.shape), lane, axis=1, mode="promise_in_bounds"
    )


def pack_kernel(state, stiff, vel, out, nodes, package, sems):
    lanes = state.shape[2]
    first = pltpu.make_async_copy(vel.at[:, 0:SHARED], nodes, sems.at[14])
    arrive = [
        pltpu.make_async_copy(state.at[c] if c < 6 else stiff, package.at[c, :, 0:lanes], sems.at[c]) for c in range(7)
    ]
    leave = [pltpu.make_async_copy(package.at[c], out.at[c], sems.at[7 + c]) for c in range(7)]
    first.start()
    for copy in arrive:
        copy.start()
    package[:, :, lanes:] = jnp.zeros((7, 8, EDGE), jnp.float32)
    first.wait()
    for c in range(3):
        for half in range(2):
            package[c, half : half + 1, lanes:] = nodes[c : c + 1, half * 128 : half * 128 + 128]
    for c in range(7):
        arrive[c].wait()
        leave[c].start()
    for copy in leave:
        copy.wait()


def is_odd():
    return lax.rem(lax.axis_index("slab"), 2) == 1


def from_previous(by_b, by_a):
    return jnp.where(is_odd(), by_a, by_b)


def from_next(by_b, by_a):
    return jnp.where(is_odd(), by_b, by_a)


def fill(d, v, k, state, stiff, got_a, got_b):
    columns = state.shape[2] // 128

    def column(j, carry):
        here = pl.ds(pl.multiple_of(j * 128, 128), 128)
        values = []
        for c in range(7):
            own = state[c, :, here] if c < 6 else stiff[:, here]
            b, a = got_b[c, :, here], got_a[c, :, here]
            values.append((from_previous(b, a), own, from_next(b, a)))
        for c in range(7):
            for slab, value in enumerate(values[c]):
                at = slab * 8
                if c < 3:
                    d[pl.ds(pl.multiple_of((c * (columns + 2) + 1 + j) * DEEP + at, 8), 8), :] = value
                elif c < 6:
                    v[pl.ds(pl.multiple_of(((c - 3) * columns + j) * DEEP + at, 8), 8), :] = value
                else:
                    k[pl.ds(pl.multiple_of(j * DEEP + at, 8), 8), :] = value
        return carry

    lax.fori_loop(0, columns, column, 0, unroll=2)
    wrap(d, columns)


def wrap(d, columns):
    for c in range(3):
        base = c * (columns + 2) * DEEP
        d[base : base + DEEP, :] = d[base + columns * DEEP : base + (columns + 1) * DEEP, :]
        end = base + (columns + 1) * DEEP
        d[end : end + DEEP, :] = d[base + DEEP : base + 2 * DEEP, :]


def advance(d, v, k, windows, columns, emit):
    lane = lax.broadcasted_iota(jnp.int32, (8, 128), 1)
    first, last = lane == 0, lane == 127

    def group(g, carry):
        def at(ref, column, row):
            start = pl.multiple_of(g * (GROUP * DEEP), 8) + (column * DEEP + row)
            return ref[pl.ds(start, 8), :]

        for w in windows:
            for c in range(3):
                ready = []
                base = c * (columns + 2)
                middles = [at(d, base + i, w) for i in range(GROUP + 2)]
                ahead = [pltpu.roll(m, 1, 1) for m in middles[:-1]]
                behind = [pltpu.roll(m, 127, 1) for m in middles[1:]]
                for i in range(GROUP):
                    left = jnp.where(first, ahead[i], ahead[i + 1])
                    right = jnp.where(last, behind[i + 1], behind[i])
                    middle = middles[i + 1]
                    above = at(d, base + i + 1, w - 1)
                    below = at(d, base + i + 1, w + 1)
                    laplace = (below + above) + (left + right) - 4.0 * middle
                    old = at(v, c * columns + i, w)
                    new = old + (at(k, i, w) * laplace - DAMPING * old)
                    ready.append((w, c, g, i, middle + new, new))
                for item in ready:
                    emit(*item)
        return carry

    lax.fori_loop(0, columns // GROUP, group, 0)


def keep(d, v, columns):
    def emit(w, c, g, i, new_d, new_v):
        base = pl.multiple_of(g * (GROUP * DEEP), 8)
        d[pl.ds(base + ((c * (columns + 2) + 1 + i) * DEEP + w), 8), :] = new_d
        v[pl.ds(base + ((c * columns + i) * DEEP + w), 8), :] = new_v

    return emit


WHOLE = [[1, 9, 15], [2, 10, 14], [3, 11, 13], [4, 12], [5, 11], [6, 10], [7, 9], [8]]


def skull_kernel(state, stiff, got_a, got_b, shared, out, send, d0, v0, d1, v1, k):
    columns = state.shape[2] // 128
    fill(d0, v0, k, state, stiff, got_a, got_b)
    now, later = (d0, v0), (d1, v1)
    for c in range(3):
        for half in range(2):
            send[c, columns + half : columns + half + 1, :] = shared[c : c + 1, half * 128 : half * 128 + 128]

    def last(w, c, g, i, new_d, new_v):
        here = pl.ds(pl.multiple_of(g * (GROUP * 128), 128) + i * 128, 128)
        out[c, :, here] = new_d
        out[3 + c, :, here] = new_v
        base = pl.multiple_of(g * (GROUP * DEEP), 8)
        v0[pl.ds(base + ((c * columns + i) * DEEP + w), 8), :] = new_v

    for step in range(SUBSTEPS):
        ends = step == SUBSTEPS - 1
        advance(*now, k, WHOLE[step], columns, last if ends else keep(*later, columns))
        if not ends:
            wrap(later[0], columns)
        now, later = later, now
        for c in range(3):
            row = now[1][pl.ds(c * columns * DEEP + 15, columns, stride=DEEP), :]
            part = ((step + 1.0) / 36.0) * row
            send[c, 0:columns, :] = part if step == 0 else send[c, 0:columns, :] + part


def prepare_kernel(vel, conn, src, weight, shear, bulk, prony, tau, corners, nodes, place, share, gains):
    regions, terms = prony.shape
    blocks = conn.shape[1] // 128
    tables = vel.shape[1] // 128
    normed = weight[...] / jnp.sum(weight[...], 0, keepdims=True)
    for half in range(2):
        place[half * 4 : half * 4 + 4, :] = src[:, half * 128 : half * 128 + 128]
        share[half * 4 : half * 4 + 4, :] = normed[:, half * 128 : half * 128 + 128]

    def put(index, value):
        gains[index * 8 : index * 8 + 8, :] = jnp.broadcast_to(value, (8, 128))

    for r in range(regions):
        put(terms * regions + r, 2.0 * shear[r])
        put((terms + 1) * regions + r, bulk[r])
    for t in range(terms):
        span = jnp.full((8, 128), tau[t], jnp.float32)
        decay = jnp.exp(-STEP_BRAIN / span)
        put((terms + 2) * regions + t, decay)
        factor = (1.0 - decay) * span / STEP_BRAIN
        for r in range(regions):
            put(t * regions + r, (2.0 * shear[r] * prony[r, t]) * factor)
    for b in range(blocks):
        nodes[pl.ds(b, 8, stride=blocks), :] = conn[:, b * 128 : b * 128 + 128]

    def block(i, carry):
        here = pl.ds(pl.multiple_of(i * 8, 8), 8)
        node = nodes[here, :]
        lane, row = node & 127, node >> 7
        found = [jnp.zeros((8, 128), jnp.float32) for _ in range(3)]
        for r in range(tables):
            mine = row == r
            for c in range(3):
                value = lookup(vel[c : c + 1, r * 128 : r * 128 + 128], lane)
                found[c] = jnp.where(mine, value, found[c])
        for c in range(3):
            corners[pl.ds(pl.multiple_of(c * 8 * blocks + i * 8, 8), 8), :] = found[c]
        return carry

    lax.fori_loop(0, blocks, block, 0)


def in_parts(value, count):
    parts = []
    for _ in range(count):
        part = value.astype(jnp.bfloat16)
        value = value - part.astype(jnp.float32)
        parts.append(part)
    return parts


def hexes_kernel(
    got_a, got_b, corners, nodes, region, vel, mass, memory_in, gains,
    memory, base, shared, scale,
    work, rate,
):
    elems = memory_in.shape[2]
    terms = memory_in.shape[0]
    regions = (gains.shape[0] // 8 - terms) // (terms + 2)
    blocks = elems // 128
    lanes = got_b.shape[2] - EDGE
    ghost = from_next(got_b[0:3, :, lanes:], got_a[0:3, :, lanes:])
    first = base.shape[1] // 128

    def add_shared(i, carry):
        node = nodes[pl.ds(pl.multiple_of(i * 8, 8), 8), :]
        lane, row = node & 127, node >> 7
        for c in range(3):
            here = pl.ds(pl.multiple_of(c * 8 * blocks + i * 8, 8), 8)
            found = corners[here, :]
            for half in range(2):
                found = jnp.where(row == first + half, lookup(ghost[c, half : half + 1], lane), found)
            work[here, :] = found
        return carry

    lax.fori_loop(0, blocks, add_shared, 0, unroll=4)

    def dense(c, q):
        return slice((c * 8 + q) * blocks, (c * 8 + q + 1) * blocks)

    slopes = []
    for c in range(3):
        v = [(0.25 * STEP_BRAIN) * work[dense(c, q), :] for q in range(8)]
        low = [v[q] + v[q + 1] for q in range(0, 8, 2)]
        along = [v[q + 1] - v[q] for q in range(0, 8, 2)]
        slopes.append(
            [
                (along[0] + along[1]) + (along[2] + along[3]),
                (low[1] - low[0]) + (low[3] - low[2]),
                (low[2] + low[3]) - (low[0] + low[1]),
            ]
        )
    strains = [slopes[c][c] for c in range(3)]
    trace = strains[0] + strains[1] + strains[2]
    devs = [strain - trace / 3.0 for strain in strains]
    devs += [0.5 * (slopes[a][b] + slopes[b][a]) for a, b in ((0, 1), (1, 2), (0, 2))]
    for i, value in enumerate(devs + [trace]):
        rate[pl.ds(i, blocks, stride=8), :] = value

    def gain(index):
        return gains[index * 8 : index * 8 + 6, :]

    normal = lax.broadcasted_iota(jnp.int32, (6, 128), 0) < 3

    def block(b, carry):
        here = pl.ds(pl.multiple_of(b * 128, 128), 128)
        mine = pl.multiple_of(b * 8, 8)
        dev = rate[pl.ds(mine, 6), :]
        trace = rate[pl.ds(mine + 6, 1), :]
        label = jnp.broadcast_to(region[:, here], (6, 128))
        masks = [label == r for r in range(regions)]

        def pick(t):
            chosen = jnp.zeros((6, 128), jnp.float32)
            for r, mask in enumerate(masks):
                chosen = jnp.where(mask, gain(t * regions + r), chosen)
            return chosen

        stress = pick(terms) * dev + jnp.where(normal, pick(terms + 1) * trace, 0.0)
        ready = []
        for t in range(terms):
            new = gain((terms + 2) * regions + t) * memory_in[t, :, here] + pick(t) * dev
            ready.append(new)
            stress = stress + new
        for t in range(terms):
            memory[t, :, here] = ready[t]
        rate[pl.ds(mine, 6), :] = jnp.where(label < regions, stress, 0.0)
        return carry

    lax.fori_loop(0, blocks, block, 0, unroll=4)
    stress = [0.25 * rate[pl.ds(i, blocks, stride=8), :] for i in range(6)]
    for c, (a, b, d) in enumerate(((0, 3, 5), (3, 1, 4), (5, 4, 2))):
        plus, minus = stress[a] + stress[b], stress[a] - stress[b]
        for q, value in ((7, plus + stress[d]), (3, plus - stress[d]), (5, minus + stress[d]), (1, minus - stress[d])):
            work[dense(c, q), :] = -value
            work[dense(c, 7 - q), :] = value

    low_rows = lax.broadcasted_iota(jnp.int32, (LO, 128), 0)
    high_rows = lax.broadcasted_iota(jnp.int32, (HI, 128), 0)

    def corner(q, sums):
        lows, parts = [], [[] for _ in range(6)]
        for b in range(blocks):
            node = nodes[pl.ds(q * blocks + b, 1), :]
            lows.append((low_rows == (node & (LO - 1))).astype(jnp.float32).astype(jnp.bfloat16))
            mine = high_rows == (node >> 7)
            for c in range(3):
                force = jnp.where(mine, work[pl.ds((c * 8 + q) * blocks + b, 1), :], 0.0)
                for p, part in enumerate(in_parts(force, 2)):
                    parts[c * 2 + p].append(part)
        left = jnp.concatenate([jnp.concatenate(row, 1) for row in parts], 0)
        return sums + lax.dot_general(
            left, jnp.concatenate(lows, 1), (((1,), (1,)), ((), ())), preferred_element_type=jnp.float32
        )

    sums = lax.fori_loop(0, 8, corner, jnp.zeros((6 * HI, LO), jnp.float32), unroll=4)
    for c in range(3):
        at = c * 2 * HI
        whole = sums[at : at + HI] + sums[at + HI : at + 2 * HI]
        for h in range(first):
            here = slice(h * LO, h * LO + LO)
            old = vel[c : c + 1, here]
            kept = 1.0 if h < first - SHARED // LO else 1.0 - COUPLING
            base[c : c + 1, here] = kept * old + STEP_BRAIN * whole[h : h + 1] / mass[:, here]
        for half in range(SHARED // LO):
            shared[c : c + 1, half * LO : half * LO + LO] = whole[first + half : first + half + 1]
    scale[...] = STEP_BRAIN / mass[:, 0:SHARED]


def finish_kernel(sent, got_a, got_b, base, scale, place, share, out):
    nodes = base.shape[1]
    tables = sent.shape[1] - 2
    lane, row = place[...] & 127, place[...] >> 7
    for c in range(3):
        before = from_previous(got_b[c], got_a[c])
        after = from_next(got_b[c], got_a[c])
        found = jnp.zeros((8, 128), jnp.float32)
        for slot, values in enumerate((before, sent[c], after)):
            for r in range(tables):
                found = jnp.where(row == slot * tables + r, lookup(values[r : r + 1], lane), found)
        found = found * share[...]
        target = jnp.concatenate(
            [jnp.sum(found[0:4], 0, keepdims=True), jnp.sum(found[4:8], 0, keepdims=True)], 1
        )
        incoming = jnp.concatenate([before[tables : tables + 1], before[tables + 1 : tables + 2]], 1)
        split = nodes - SHARED
        out[c : c + 1, 0:SHARED] = base[c : c + 1, 0:SHARED] + incoming * scale[...]
        out[c : c + 1, SHARED:split] = base[c : c + 1, SHARED:split]
        out[c : c + 1, split:] = base[c : c + 1, split:] + COUPLING * target


def on_device(
    skull_state, stiffness, intersection_src, intersection_weight, brain_vel, connectivity, region,
    shear_table, bulk_table, prony_weight, prony_tau, prony_state, node_mass,
):
    lanes = skull_state.shape[2]
    columns = lanes // 128
    nodes = brain_vel.shape[1]
    elems = connectivity.shape[1]
    terms, regions = prony_weight.shape
    count = lax.axis_size("slab")
    vmem = pl.BlockSpec(memory_space=pltpu.VMEM)
    smem = pl.BlockSpec(memory_space=pltpu.SMEM)
    hbm = pl.BlockSpec(memory_space=pltpu.HBM)
    shape = lambda *dims: jax.ShapeDtypeStruct(dims, jnp.float32)
    scratch = lambda *dims: pltpu.VMEM(dims, jnp.float32)

    def kernel(body, out, operands, results, scratch_shapes=(), flops=1_000_000, vmem_mib=32):
        return pl.pallas_call(
            body,
            out_shape=out,
            in_specs=operands,
            out_specs=results,
            scratch_shapes=list(scratch_shapes),
            compiler_params=pltpu.CompilerParams(vmem_limit_bytes=vmem_mib << 20),
            cost_estimate=pl.CostEstimate(flops=flops, bytes_accessed=4_000_000, transcendentals=0),
            name=body.__name__.removesuffix("_kernel"),
        )

    swap_a = [(i, i ^ 1) for i in range(count)]
    swap_b = [(i, ((i + 1) ^ 1) - 1) for i in range(1, count - 1)]

    def swap(value):
        return lax.ppermute(value, "slab", swap_b), lax.ppermute(value, "slab", swap_a)

    field = [scratch(3 * (columns + 2) * DEEP, 128), scratch(3 * columns * DEEP, 128)]
    slabs = field + field + [scratch(columns * DEEP, 128)]

    package = kernel(
        pack_kernel, shape(7, 8, lanes + EDGE), [hbm, hbm, hbm], hbm,
        [scratch(3, SHARED), scratch(7, 8, lanes + EDGE), pltpu.SemaphoreType.DMA((15,))], vmem_mib=60,
    )(skull_state, stiffness, brain_vel)
    got_b, got_a = swap(package)
    gain_rows = ((terms + 2) * regions + terms) * 8
    index = lambda *dims: jax.ShapeDtypeStruct(dims, jnp.int32)
    blocks = elems // 128
    corners, dense_nodes, place, share, gains = kernel(
        prepare_kernel,
        (shape(24 * blocks, 128), index(8 * blocks, 128), index(8, 128), shape(8, 128), shape(gain_rows, 128)),
        [vmem] * 4 + [smem] * 4,
        [vmem] * 5,
    )(
        brain_vel, connectivity, intersection_src.T, intersection_weight.T,
        shear_table, bulk_table, prony_weight.T, prony_tau,
    )
    memory, base, shared, scale = kernel(
        hexes_kernel,
        (shape(*prony_state.shape), shape(3, nodes), shape(3, SHARED), shape(1, SHARED)),
        [vmem] * 9,
        [vmem] * 4,
        [scratch(24 * blocks, 128), scratch(8 * blocks, 128)],
    )(
        got_a, got_b, corners, dense_nodes, region.reshape(1, elems),
        brain_vel, node_mass.reshape(1, nodes), prony_state, gains,
    )
    skull_out, sent = kernel(
        skull_kernel,
        (shape(*skull_state.shape), shape(3, columns + 2, 128)),
        [vmem] * 5,
        [vmem] * 2,
        slabs,
    )(skull_state, stiffness, got_a, got_b, shared)
    back_b, back_a = swap(sent)
    brain_out = kernel(finish_kernel, shape(3, nodes), [vmem] * 7, vmem)(
        sent, back_a, back_b, base, scale, place, share
    )
    return skull_out, brain_out, memory


def solution(mesh):
    placed = (
        P(None, "slab", None),
        P("slab", None),
        P("slab", None),
        P("slab", None),
        P(None, "slab"),
        P(None, "slab"),
        P("slab"),
        P(),
        P(),
        P(),
        P(),
        P(None, None, "slab"),
        P("slab"),
    )
    return jax.shard_map(
        on_device,
        mesh=mesh,
        in_specs=placed,
        out_specs=(P(None, "slab", None), P(None, "slab"), P(None, None, "slab")),
        check_vma=False,
    )
```
